32 devices in a mesh: dp: 8 (over z, core), seq: 4 (over y, x).
Axes of the slice: x: 2, y: 2, z: 4, core: 2. Of those that a mesh axis runs over, the one named last changes fastest.
Arguments:
- inputs: bfloat16 [8, 1024, 1024], P('dp', 'seq'), may hold values from -6 to 6
- segments: int32 [8, 1024], P('dp'), may hold values from 0 to 8, as said below
- cotangent: bfloat16 [8, 1024, 1024], P('dp', 'seq'), may hold values from -6 to 6
- mixer_gate: bfloat16 [1024, 1536], P(('dp', 'seq')), may hold values from -0.1875 to 0.1875
- mixer_input: bfloat16 [1024, 1792], P(('dp', 'seq')), may hold values from -0.1875 to 0.1875
- mixer_step: bfloat16 [1024, 24], P(('dp', 'seq')), may hold values from -0.1875 to 0.1875
- mixer_output: bfloat16 [1536, 1024], P(('dp', 'seq')), may hold values from -0.15625 to 0.15625
- query_weight: bfloat16 [1024, 512], P(('dp', 'seq')), may hold values from -0.1875 to 0.1875
- key_weight: bfloat16 [1024, 128], P(('dp', 'seq')), may hold values from -0.1875 to 0.1875
- value_weight: bfloat16 [1024, 128], P(('dp', 'seq')), may hold values from -0.1875 to 0.1875
- output_weight: bfloat16 [512, 1024], P(('dp', 'seq')), may hold values from -1.5 to 1.5
- gate_weight: bfloat16 [1024, 2048], P(('dp', 'seq')), may hold values from -0.1875 to 0.1875
- up_weight: bfloat16 [1024, 2048], P(('dp', 'seq')), may hold values from -0.1875 to 0.1875
- down_weight: bfloat16 [2048, 1024], P(('dp', 'seq')), may hold values from -0.125 to 0.125
- input_gain: float32 [1024], replicated, may hold values from 0.25 to 1.75
- second_gain: float32 [1024], replicated, may hold values from 0.25 to 1.75
- mixer_gain: float32 [1536], replicated, may hold values from 0.25 to 1.75
- filter_taps: float32 [4, 1792], replicated, may hold values from -3 to 3
- filter_bias: float32 [1792], replicated, may hold values from -3 to 3
- decay_log: float32 [24], replicated, may hold values from -7.5 to -3
- step_bias: float32 [24], replicated, may hold values from -1 to 1
- skip_gain: float32 [24], replicated, may hold values from 0.5 to 1.5
Outputs:
- result: bfloat16 [8, 1024, 1024], P('dp', 'seq')
- input_grad: float32 [8, 1024, 1024], P('dp', 'seq')
- grad_mixer_gate: float32 [1024, 1536], P(('dp', 'seq'))
- grad_mixer_input: float32 [1024, 1792], P(('dp', 'seq'))
- grad_mixer_step: float32 [1024, 24], P(('dp', 'seq'))
- grad_mixer_output: float32 [1536, 1024], P(('dp', 'seq'))
- grad_query: float32 [1024, 512], P(('dp', 'seq'))
- grad_key: float32 [1024, 128], P(('dp', 'seq'))
- grad_value: float32 [1024, 128], P(('dp', 'seq'))
- grad_output: float32 [512, 1024], P(('dp', 'seq'))
- grad_gate: float32 [1024, 2048], P(('dp', 'seq'))
- grad_up: float32 [1024, 2048], P(('dp', 'seq'))
- grad_down: float32 [2048, 1024], P(('dp', 'seq'))
- grad_input_gain: float32 [1024], replicated
- grad_second_gain: float32 [1024], replicated
- grad_mixer_gain: float32 [1536], replicated
- grad_filter_taps: float32 [4, 1792], replicated
- grad_filter_bias: float32 [1792], replicated
- grad_decay_log: float32 [24], replicated
- grad_step_bias: float32 [24], replicated
- grad_skip_gain: float32 [24], replicated
The draws below stay inside these ranges and needn't reach their ends.
Inputs may be any that keep to these rules, and one draw needn't show every extreme that they name: `segments`: in each sequence the segment numbers start at 0 and never fall; in one sequence, drawn from the seed, all 1024 tokens form one document.
All inputs are finite; a program needn't handle non-finite values.
Results may differ from the reference program's by a relative error of at most 0.014.
Values may be sent and summed in bfloat16 or wider, within the bound.
No kernel may reach another device: no remote copies, remote signals or barrier semaphores. Data moves between devices by JAX's collectives and lax.ppermute only.
A program may use at most 256 MiB of HBM per device.

```python
import jax
import jax.numpy as jnp
from jax import lax

D = 1024
HEADS = 8
KV_HEADS = 2
HEAD = 64
SSM_HEADS = 24
SSM_HEAD = 64
STATE = 128
CONV = 4
FF = 2048
SEQ_LEN = 1024
TOK_DEV = 256
SEQS = 8
INNER = 1536
XBC = 1792


def draw_segments(key, part):
    key = jax.random.fold_in(key, 11)
    key_cuts, key_whole = jax.random.split(key)
    cut_points = jax.random.randint(key_cuts, (SEQS, 8), 1, SEQ_LEN)
    whole_row = jax.random.randint(key_whole, (), 0, SEQS)
    position = jnp.arange(SEQ_LEN)
    numbers = jnp.sum((position[None, None, :] >= cut_points[:, :, None]).astype(jnp.int32), axis=1)
    keep_rows = (jnp.arange(SEQS) != whole_row).astype(jnp.int32)
    return (numbers * keep_rows[:, None]).astype(jnp.int32)


def steps_of(rng, extent, cuts, low, high):
    def one(axis_at, parts):
        heights = jax.random.uniform(jax.random.fold_in(jax.random.fold_in(rng, 6), axis_at), (parts,), jnp.float32, low / len(cuts), high / len(cuts))
        return jnp.repeat(jnp.exp(heights), extent[axis_at] // parts).reshape((-1,) + (1,) * (len(extent) - axis_at - 1))

    level = one(*cuts[0])
    for cut in cuts[1:]:
        level = level * one(*cut)
    return level


def bell_draw(rng, extent, deviation, bound, cuts=(), held_as=jnp.bfloat16):
    factor_of = steps_of(rng, extent, cuts, -0.22, 0.18) if cuts else 1.0
    drawn = jax.random.normal(rng, extent, jnp.float32) * deviation * factor_of
    return jnp.minimum(jnp.maximum(drawn, -bound), bound).astype(held_as)


def setup_inputs(seed: int = 0) -> dict:
    key_of = jax.random.split(jax.random.key(seed), 23)
    return {
        "inputs": bell_draw(key_of[0], (SEQS, SEQ_LEN, D), 1.0, 6.0, ((0, 8), (1, 4))),
        "segments": draw_segments(jax.random.fold_in(key_of[22], 71), 0),
        "cotangent": bell_draw(key_of[2], (SEQS, SEQ_LEN, D), 1.0, 6.0, ((0, 8), (1, 4))),
        "mixer_gate": bell_draw(key_of[3], (D, INNER), D ** -0.5, 0.1875, ((0, 32),)),
        "mixer_input": bell_draw(key_of[4], (D, XBC), D ** -0.5, 0.1875, ((0, 32),)),
        "mixer_step": bell_draw(key_of[5], (D, SSM_HEADS), D ** -0.5, 0.1875, ((0, 32),)),
        "mixer_output": bell_draw(key_of[6], (INNER, D), INNER ** -0.5, 0.15625, ((0, 32),)),
        "query_weight": bell_draw(key_of[7], (D, HEADS * HEAD), D ** -0.5, 0.1875, ((0, 32),)),
        "key_weight": bell_draw(key_of[8], (D, KV_HEADS * HEAD), D ** -0.5, 0.1875, ((0, 32),)),
        "value_weight": bell_draw(key_of[9], (D, KV_HEADS * HEAD), D ** -0.5, 0.1875, ((0, 32),)),
        "output_weight": bell_draw(key_of[10], (HEADS * HEAD, D), 16 ** -0.5, 1.5, ((0, 32),)),
        "gate_weight": bell_draw(key_of[11], (D, FF), D ** -0.5, 0.1875, ((0, 32),)),
        "up_weight": bell_draw(key_of[12], (D, FF), D ** -0.5, 0.1875, ((0, 32),)),
        "down_weight": bell_draw(key_of[13], (FF, D), FF ** -0.5, 0.125, ((0, 32),)),
        "input_gain": jnp.clip(1.0 + 0.15 * jax.random.normal(key_of[14], (D,), jnp.float32), 0.25, 1.75),
        "second_gain": jnp.clip(1.0 + 0.15 * jax.random.normal(key_of[15], (D,), jnp.float32), 0.25, 1.75),
        "mixer_gain": jnp.clip(1.0 + 0.15 * jax.random.normal(key_of[16], (INNER,), jnp.float32), 0.25, 1.75),
        "filter_taps": bell_draw(key_of[17], (CONV, XBC), 0.5, 3.0, (), jnp.float32),
        "filter_bias": bell_draw(key_of[18], (XBC,), 0.5, 3.0, (), jnp.float32),
        "decay_log": jnp.clip(jax.random.uniform(key_of[19], (SSM_HEADS,), jnp.float32, -7.5, -3.0), -7.5, -3.0),
        "step_bias": jnp.clip(jax.random.uniform(key_of[20], (SSM_HEADS,), jnp.float32, -1.0, 1.0), -1.0, 1.0),
        "skip_gain": jnp.clip(jax.random.uniform(key_of[21], (SSM_HEADS,), jnp.float32, 0.5, 1.5), 0.5, 1.5),
    }


eps = 1e-05
rope_theta = 100000000000.0
score_scale = 0.125

@jax.custom_vjp
def low(v):
    return lax.optimization_barrier(v.astype(jnp.bfloat16)).astype(jnp.float32)

@jax.custom_vjp
def low_back(v):
    return v

def low_keep(v):
    return (low(v), None)

def low_pass(kept, grad):
    return (grad,)

def back_keep(v):
    return (v, None)

def back_low(kept, grad):
    return (low(grad),)
low.defvjp(low_keep, low_pass)
low_back.defvjp(back_keep, back_low)

def hdot(left, right):
    return jnp.dot(left, right, precision=lax.Precision.HIGHEST, preferred_element_type=jnp.float32)

def rms_scale(tensor, scale_gain):
    return tensor * lax.rsqrt(lax.optimization_barrier(jnp.mean(tensor * tensor, axis=-1, keepdims=True)) + eps) * scale_gain

def rotate(tensor, positions, direction):
    half_width = tensor.shape[-1] // 2
    frequency = rope_theta ** (-jnp.arange(half_width, dtype=jnp.float32) / half_width)
    angle = positions.astype(jnp.float32)[:, None] * frequency[None, :]
    cosine = jnp.cos(angle)[:, None, :]
    sine_part = direction * jnp.sin(angle)[:, None, :]
    first_half = tensor[..., :half_width]
    second_half = tensor[..., half_width:]
    return jnp.concatenate([first_half * cosine - second_half * sine_part, second_half * cosine + first_half * sine_part], axis=-1)

def conv_apply(extended, ext_segments, filter_taps, filter_bias):
    length = extended.shape[0] - CONV + 1
    own_segment = ext_segments[CONV - 1:]
    summed = jnp.zeros((length, extended.shape[1]), jnp.float32) + filter_bias[None, :]
    for offset in range(CONV):
        match_mask = (ext_segments[offset:offset + length] == own_segment).astype(jnp.float32)[:, None]
        summed = summed + filter_taps[offset][None, :] * extended[offset:offset + length] * match_mask
    return jax.nn.silu(summed)

def ssd_split(filtered, step_raw, step_bias, decay_log):
    length = filtered.shape[0]
    inner = SSM_HEADS * SSM_HEAD
    values = filtered[:, :inner].reshape(length, SSM_HEADS, SSM_HEAD)
    write_map = filtered[:, inner:inner + STATE]
    read_map = filtered[:, inner + STATE:]
    stride = jax.nn.softplus(step_raw + step_bias)
    running = jnp.cumsum(stride * -jnp.exp(decay_log), axis=0)
    return (values, write_map, read_map, stride, running)

def ssd_state(filtered, step_raw, step_bias, decay_log, doc_ids, seg_prior):
    values, write_map, read_map, stride, running = ssd_split(filtered, step_raw, step_bias, decay_log)
    final_log = running[-1]
    keep_end = (doc_ids == doc_ids[-1]).astype(jnp.float32)[:, None]
    end_weights = jnp.exp(final_log[None, :] - running) * keep_end * stride
    end_state = jnp.einsum('th,thd,tn->hdn', end_weights, values, write_map, precision=lax.Precision.HIGHEST)
    decay_total = jnp.exp(final_log) * (doc_ids[-1] == seg_prior).astype(jnp.float32)
    return (decay_total, end_state)

def ssd_output(filtered, step_raw, step_bias, decay_log, skip_gain, doc_ids, seg_prior, start_state):
    values, write_map, read_map, stride, running = ssd_split(filtered, step_raw, step_bias, decay_log)
    length = filtered.shape[0]
    token_order = jnp.arange(length)
    allowed = (token_order[:, None] >= token_order[None, :]) & (doc_ids[:, None] == doc_ids[None, :])
    gap_logs = running.T[:, :, None] - running.T[:, None, :]
    decay_mat = jnp.where(allowed[None], jnp.exp(jnp.minimum(gap_logs, 0.0)), 0.0)
    inner_prod = jnp.dot(read_map, write_map.T, precision=lax.Precision.HIGHEST)
    mixing = decay_mat * inner_prod[None] * stride.T[:, None, :]
    local_part = jnp.einsum('hts,shd->thd', mixing, values, precision=lax.Precision.HIGHEST)
    entering = (doc_ids == seg_prior).astype(jnp.float32)[:, None] * jnp.exp(running)
    carried = jnp.einsum('hdn,tn->thd', start_state, read_map, precision=lax.Precision.HIGHEST) * entering[:, :, None]
    summed = local_part + carried + skip_gain[None, :, None] * values
    return summed.reshape(length, SSM_HEADS * SSM_HEAD)

def gated_norm(ssm_out, gate_mix, mixer_gain):
    return rms_scale(ssm_out * jax.nn.silu(gate_mix), mixer_gain)

def mamba_stretches(filtered, step_raw, step_bias, decay_log, skip_gain, doc_ids):
    length = filtered.shape[0]
    before = jnp.concatenate([jnp.full((1,), -1, jnp.int32), doc_ids[TOK_DEV - 1::TOK_DEV][:-1]])

    def advance(state_now, pieces):
        xc_piece, step_piece, seg_piece, seg_prior = pieces
        decay_total, end_state = ssd_state(xc_piece, step_piece, step_bias, decay_log, seg_piece, seg_prior)
        outputs = ssd_output(xc_piece, step_piece, step_bias, decay_log, skip_gain, seg_piece, seg_prior, state_now)
        return (decay_total[:, None, None] * state_now + end_state, outputs)
    start_state = jnp.zeros((SSM_HEADS, SSM_HEAD, STATE), jnp.float32)
    pieces = (filtered.reshape(length // TOK_DEV, TOK_DEV, filtered.shape[1]), step_raw.reshape(length // TOK_DEV, TOK_DEV, SSM_HEADS), doc_ids.reshape(length // TOK_DEV, TOK_DEV), before)
    final_state, pieces_out = lax.scan(jax.checkpoint(advance), start_state, pieces)
    return pieces_out.reshape(length, SSM_HEADS * SSM_HEAD)

def one_sequence(doc_ids, tokens, params):
    mixer_gate, mixer_input, mixer_step, mixer_output, query_weight, key_weight, value_weight, output_weight, gate_weight, up_weight, down_weight, input_gain, second_gain, mixer_gain, filter_taps, filter_bias, decay_log, step_bias, skip_gain = params
    length = tokens.shape[0]
    positions = jnp.arange(length)
    normed = low(rms_scale(tokens, input_gain))
    gate_mix = low_back(hdot(normed, mixer_gate))
    mixed_raw = low(low_back(hdot(normed, mixer_input)))
    step_raw = low_back(hdot(normed, mixer_step))
    queries = low_back(hdot(normed, query_weight))
    keys_raw = low_back(hdot(normed, key_weight))
    values_low = low(low_back(hdot(normed, value_weight)))
    extended = jnp.concatenate([jnp.zeros((CONV - 1, mixed_raw.shape[1]), jnp.float32), mixed_raw], axis=0)
    ext_segments = jnp.concatenate([jnp.full((CONV - 1,), -1, jnp.int32), doc_ids])
    filtered = low(conv_apply(extended, ext_segments, filter_taps, filter_bias))
    ssm_out = mamba_stretches(filtered, step_raw, step_bias, decay_log, skip_gain, doc_ids)
    gated_out = low(gated_norm(ssm_out, gate_mix, mixer_gain))
    mixer_result = low_back(hdot(gated_out, mixer_output))
    query_rot = low(rotate(queries.reshape(length, HEADS, HEAD), positions, 1.0))
    key_rot = low(rotate(keys_raw.reshape(length, KV_HEADS, HEAD), positions, 1.0))
    repeat = HEADS // KV_HEADS
    key_full = jnp.repeat(key_rot, repeat, axis=1)
    value_full = jnp.repeat(values_low.reshape(length, KV_HEADS, HEAD), repeat, axis=1)
    scores = low_back(jnp.einsum('qhd,khd->hqk', query_rot, key_full, precision=lax.Precision.HIGHEST) * score_scale)
    allowed = (positions[:, None] >= positions[None, :]) & (doc_ids[:, None] == doc_ids[None, :])
    scores = jnp.where(allowed[None], scores, -1e+30)
    probs = low(jax.nn.softmax(scores, axis=-1))
    attended = jnp.einsum('hqk,khd->qhd', probs, value_full, precision=lax.Precision.HIGHEST).reshape(length, HEADS * HEAD)
    attended = low_back(low(attended))
    attn_result = low_back(hdot(attended, output_weight))
    middle = tokens + attn_result + mixer_result
    second = low(rms_scale(middle, second_gain))
    gate_val = low_back(hdot(second, gate_weight))
    up_val = low_back(hdot(second, up_weight))
    activated = low(jax.nn.silu(gate_val) * up_val)
    return middle + low_back(hdot(activated, down_weight))

def forward(doc_table, tokens, params):

    def per_sequence(seq_pair):
        return one_sequence(seq_pair[1], seq_pair[0], params)
    return lax.map(jax.checkpoint(per_sequence), (tokens, doc_table))

def reference(inputs, segments, cotangent, mixer_gate, mixer_input, mixer_step, mixer_output, query_weight, key_weight, value_weight, output_weight, gate_weight, up_weight, down_weight, input_gain, second_gain, mixer_gain, filter_taps, filter_bias, decay_log, step_bias, skip_gain):
    params = tuple((piece.astype(jnp.float32) for piece in (mixer_gate, mixer_input, mixer_step, mixer_output, query_weight, key_weight, value_weight, output_weight, gate_weight, up_weight, down_weight, input_gain, second_gain, mixer_gain, filter_taps, filter_bias, decay_log, step_bias, skip_gain)))

    def wrapped(tokens, weights):
        return forward(segments, tokens, weights)
    result, pullback = jax.vjp(wrapped, inputs.astype(jnp.float32), params)
    token_grad, param_grads = pullback(cotangent.astype(jnp.float32))
    return (result.astype(jnp.bfloat16), token_grad, param_grads[0], param_grads[1], param_grads[2], param_grads[3], param_grads[4], param_grads[5], param_grads[6], param_grads[7], param_grads[8], param_grads[9], param_grads[10], param_grads[11], param_grads[12], param_grads[13], param_grads[14], param_grads[15], param_grads[16], param_grads[17], param_grads[18])
```

```python
import jax
import jax.numpy as jnp
from jax import lax
from jax.sharding import PartitionSpec as P

HEADS = 8
KV_HEADS = 2
HEAD = 64
SSM_HEADS = 24
SSM_HEAD = 64
STATE = 128
CONV = 4


eps = 1e-05
rope_theta = 100000000000.0
score_scale = 0.125


def passed_along(x, axis, by):
    length = lax.axis_size(axis)
    pairs = [(i, i + by) for i in range(length) if 0 <= i + by < length]
    return lax.ppermute(x, axis, pairs)


def matmul(left, right):
    return jnp.dot(left, right, preferred_element_type=jnp.float32)


def rows_product(left, right):
    return lax.dot_general(
        left, right, (((0,), (0,)), ((), ())), preferred_element_type=jnp.float32
    )


def back_product(left, right):
    return lax.dot_general(
        left, right, (((1,), (1,)), ((), ())), preferred_element_type=jnp.float32
    )


def rms_scale(tensor, scale_gain):
    return tensor * lax.rsqrt(jnp.mean(tensor * tensor, axis=-1, keepdims=True) + eps) * scale_gain


def rotate(tensor, positions, direction):
    half_width = tensor.shape[-1] // 2
    frequency = rope_theta ** (-jnp.arange(half_width, dtype=jnp.float32) / half_width)
    angle = positions.astype(jnp.float32)[:, None] * frequency[None, :]
    cosine = jnp.cos(angle)[:, None, :]
    sine_part = direction * jnp.sin(angle)[:, None, :]
    first_half = tensor[..., :half_width]
    second_half = tensor[..., half_width:]
    return jnp.concatenate(
        [
            first_half * cosine - second_half * sine_part,
            second_half * cosine + first_half * sine_part,
        ],
        axis=-1,
    )


def conv_apply(extended, ext_segments, filter_taps, filter_bias):
    length = extended.shape[0] - CONV + 1
    own_segment = ext_segments[CONV - 1 :]
    summed = jnp.zeros((length, extended.shape[1]), jnp.float32) + filter_bias[None, :]
    for offset in range(CONV):
        match_mask = (ext_segments[offset : offset + length] == own_segment).astype(jnp.float32)[
            :, None
        ]
        summed = (
            summed + filter_taps[offset][None, :] * extended[offset : offset + length] * match_mask
        )
    return jax.nn.silu(summed)


def running_sum(x):
    order = jnp.arange(x.shape[0])
    earlier = (order[:, None] >= order[None, :]).astype(jnp.float32)
    return jnp.dot(earlier, x, precision=lax.Precision.HIGHEST)


def ssd_split(filtered, step_raw, step_bias, decay_log):
    length = filtered.shape[0]
    inner = SSM_HEADS * SSM_HEAD
    values = filtered[:, :inner].reshape(length, SSM_HEADS, SSM_HEAD)
    write_map = filtered[:, inner : inner + STATE]
    read_map = filtered[:, inner + STATE :]
    stride = jax.nn.softplus(step_raw + step_bias)
    running = running_sum(stride * -jnp.exp(decay_log))
    return (values, write_map, read_map, stride, running)


def ssd_state(filtered, step_raw, step_bias, decay_log, doc_ids, seg_prior):
    values, write_map, read_map, stride, running = ssd_split(
        filtered, step_raw, step_bias, decay_log
    )
    final_log = running[-1]
    keep_end = (doc_ids == doc_ids[-1]).astype(jnp.float32)[:, None]
    end_weights = jnp.exp(final_log[None, :] - running) * keep_end * stride
    end_state = jnp.einsum(
        "th,thd,tn->hdn", end_weights, values, write_map, precision=lax.Precision.HIGHEST
    )
    decay_total = jnp.exp(final_log) * (doc_ids[-1] == seg_prior).astype(jnp.float32)
    return (decay_total, end_state)


def ssd_output(
    filtered, step_raw, step_bias, decay_log, skip_gain, doc_ids, seg_prior, start_state
):
    values, write_map, read_map, stride, running = ssd_split(
        filtered, step_raw, step_bias, decay_log
    )
    length = filtered.shape[0]
    token_order = jnp.arange(length)
    allowed = (token_order[:, None] >= token_order[None, :]) & (
        doc_ids[:, None] == doc_ids[None, :]
    )
    gap_logs = running.T[:, :, None] - running.T[:, None, :]
    decay_mat = jnp.where(allowed[None], jnp.exp(jnp.minimum(gap_logs, 0.0)), 0.0)
    inner_prod = jnp.dot(read_map, write_map.T, precision=lax.Precision.HIGHEST)
    mixing = decay_mat * inner_prod[None] * stride.T[:, None, :]
    local_part = jnp.einsum("hts,shd->thd", mixing, values, precision=lax.Precision.HIGHEST)
    entering = (doc_ids == seg_prior).astype(jnp.float32)[:, None] * jnp.exp(running)
    carried = (
        jnp.einsum("hdn,tn->thd", start_state, read_map, precision=lax.Precision.HIGHEST)
        * entering[:, :, None]
    )
    summed = local_part + carried + skip_gain[None, :, None] * values
    return summed.reshape(length, SSM_HEADS * SSM_HEAD)


def gated_norm(ssm_out, gate_mix, mixer_gain):
    return rms_scale(ssm_out * jax.nn.silu(gate_mix), mixer_gain)


def swiglu(gate_val, up_val):
    return jax.nn.silu(gate_val) * up_val


def shift_along(x, line, by):
    axis, stride, size = line
    pairs = []
    for index in range(lax.axis_size(axis)):
        place = (index // stride) % size
        pairs.append((index, index + ((place + by) % size - place) * stride))
    return lax.ppermute(x, axis, pairs)


def mesh_lines():
    replicas, pieces = (lax.axis_size("dp"), lax.axis_size("seq"))
    across = 1
    while across * across * 2 <= pieces:
        across *= 2
    lines = {
        "core": ("dp", 1, 2),
        "z": ("dp", 2, replicas // 2),
        "x": ("seq", 1, across),
        "y": ("seq", across, pieces // across),
    }
    return lines


def place_on(line):
    axis, stride, size = line
    return (lax.axis_index(axis) // stride) % size


def tie(*groups):
    return lax.optimization_barrier(groups)


def gather_levels(packed, lines):
    return [packed] + [shift_along(packed, lines["z"], -d) for d in range(1, lines["z"][2])]


def spread(levels, cut, lines):
    owns = []
    for y_last in (True, False):
        first, second = ("x", "y") if y_last else ("y", "x")
        first_size, second_size = (lines[first][2], lines[second][2])
        part = jnp.concatenate([a[:, :cut] if y_last else a[:, cut:] for a in levels], axis=0)
        near = [part] + [shift_along(part, lines[first], -d) for d in range(1, first_size)]
        near = jnp.concatenate(near, axis=0)
        far = [near] + [shift_along(near, lines[second], -d) for d in range(1, second_size)]
        rows = part.shape[0]
        blocks = []
        for y in range(lines["y"][2]):
            for x in range(lines["x"][2]):
                outer, at = (y, x) if y_last else (x, y)
                blocks.append(far[outer][at * rows : (at + 1) * rows])
        owns.append(jnp.concatenate(blocks, axis=0))
    return [(own, shift_along(own, lines["core"], 1)) for own in owns]


def relative_index(row_counts, lines):
    levels, rows_out, across = (lines["z"][2], lines["y"][2], lines["x"][2])
    total = sum(row_counts)
    places = []
    start = 0
    for rows in row_counts:
        column = jnp.arange(levels * 2 * rows_out * across * rows)
        row = column % rows
        device = column // rows
        x = (device % across - place_on(lines["x"])) % across
        y = (device // across % rows_out - place_on(lines["y"])) % rows_out
        core = (device // (across * rows_out) - place_on(lines["core"])) % 2
        level = (device // (across * rows_out * 2) - place_on(lines["z"])) % levels
        block = ((core * rows_out + y) * across + x) * levels + level
        places.append(block * total + start + row)
        start += rows
    return jnp.concatenate(places) if len(places) > 1 else places[0]


def permutation(row_counts, lines):
    index = relative_index(row_counts, lines)
    return (index[:, None] == jnp.arange(index.shape[0])[None, :]).astype(jnp.bfloat16)


def to_relative(low, order):
    return matmul(low, order).astype(jnp.bfloat16)


def from_relative(wide, order):
    high = lax.reduce_precision(wide, 8, 7)
    rest = wide - high
    return back_product(high.astype(jnp.bfloat16), order) + back_product(
        rest.astype(jnp.bfloat16), order
    )


def product_rel(low_rel, weights):
    own, other = weights
    half = own.shape[0]
    return matmul(low_rel[:, :half], own) + matmul(low_rel[:, half:], other)


def back_rel(grad, weights):
    own, other = weights
    return jnp.concatenate([back_product(grad, own), back_product(grad, other)], axis=1)


def owed(items, lines):
    rows_out, across, levels = (lines["y"][2], lines["x"][2], lines["z"][2])
    theirs = []
    if items[0][0] is items[1][0]:
        left = items[0][0]
        grad = jnp.concatenate([items[0][1], items[1][1]], axis=1)
        theirs.append(rows_product(left[:, left.shape[1] // 2 :], grad).astype(jnp.bfloat16))
    else:
        for left, grad in items:
            theirs.append(rows_product(left[:, left.shape[1] // 2 :], grad).astype(jnp.bfloat16))
    received = [shift_along(part, lines["core"], 1) for part in theirs]
    received = yield received
    if len(received) == 1:
        width = items[0][1].shape[1]
        received = [received[0][:, :width], received[0][:, width:]]
    kept = []
    arrived = []
    for (left, grad), add, y_first in zip(items, received, (True, False)):
        first, second = ("y", "x") if y_first else ("x", "y")
        first_size, second_size = (lines[first][2], lines[second][2])
        block = left.shape[1] // 2 // (rows_out * across)

        def of_first(i):
            ids = [(i * across + j) if y_first else (j * across + i) for j in range(second_size)]
            rows = jnp.concatenate([left[:, k * block : (k + 1) * block] for k in ids], axis=1)
            more = jnp.concatenate([add[k * block : (k + 1) * block] for k in ids], axis=0)
            return rows_product(rows, grad) + more.astype(jnp.float32)

        kept.append(of_first(0))
        arrived.append(
            [
                shift_along(of_first(i).astype(jnp.bfloat16), lines[first], i)
                for i in range(1, first_size)
            ]
        )
    arrived = yield arrived
    sums = []
    sent = []
    for own, others, (left, grad), y_first in zip(kept, arrived, items, (True, False)):
        second = lines["x" if y_first else "y"]
        block = own.shape[0] // second[2]

        def of_second(j):
            summed = own[j * block : (j + 1) * block]
            for other in others:
                summed = summed + other[j * block : (j + 1) * block].astype(jnp.float32)
            return summed

        sums.append(of_second(0))
        sent.append(
            [
                shift_along(of_second(j).astype(jnp.bfloat16), second, j)
                for j in range(1, second[2])
            ]
        )
    sent = yield sent

    def of_level(k):
        parts = []
        for own, others in zip(sums, sent):
            rows = own.shape[0] // levels
            summed = own[k * rows : (k + 1) * rows]
            for other in others:
                summed = summed + other[k * rows : (k + 1) * rows].astype(jnp.float32)
            parts.append(summed)
        return jnp.concatenate(parts, axis=1)

    last = [
        shift_along(of_level(k).astype(jnp.bfloat16), lines["z"], k) for k in range(1, levels)
    ]
    last = yield last
    total = of_level(0)
    for part in last:
        total = total + part.astype(jnp.float32)
    width = items[0][1].shape[1]
    yield [total[:, :width], total[:, width:]]


def sum_everywhere(x):
    for axis in ("dp", "seq"):
        size = lax.axis_size(axis)
        step = 1
        while step < size:
            x = x + lax.ppermute(x, axis, [(i, i ^ step) for i in range(size)])
            step *= 2
    return x


def from_earlier(x, by):
    return passed_along(x, "seq", by)


def body(
    inputs,
    segments,
    cotangent,
    mixer_gate,
    mixer_input,
    mixer_step,
    mixer_output,
    query_weight,
    key_weight,
    value_weight,
    output_weight,
    gate_weight,
    up_weight,
    down_weight,
    input_gain,
    second_gain,
    mixer_gain,
    filter_taps,
    filter_bias,
    decay_log,
    step_bias,
    skip_gain,
):
    piece_index = lax.axis_index("seq")
    local_len = inputs.shape[1]
    seq_len = segments.shape[1]
    first_token = piece_index * local_len
    all_segs = segments[0]
    own_segments = lax.dynamic_slice_in_dim(all_segs, first_token, local_len)
    rim_start = jnp.maximum(first_token - (CONV - 1), 0)
    rim_segments = jnp.where(
        piece_index > 0, lax.dynamic_slice_in_dim(all_segs, rim_start, CONV - 1), -1
    )
    seg_before = rim_segments[CONV - 2]
    positions = first_token + jnp.arange(local_len)
    ext_segments = jnp.concatenate([rim_segments, own_segments])
    pieces = lax.axis_size("seq")
    lines = mesh_lines()
    inner = SSM_HEADS * SSM_HEAD
    query_width = HEADS * HEAD
    key_width = KV_HEADS * HEAD
    conv_width = mixer_input.shape[1]
    step_pad = jnp.pad(mixer_step, ((0, 0), (0, 128 - SSM_HEADS)))
    packed_first = jnp.concatenate(
        [mixer_gate, query_weight, step_pad, mixer_input, key_weight, value_weight], axis=1
    )
    first_cut = inner + query_width + step_pad.shape[1]
    packed_branch = jnp.concatenate(
        [jnp.concatenate([mixer_output, output_weight], axis=0), down_weight], axis=1
    )
    packed_up = jnp.concatenate([gate_weight, up_weight], axis=1)
    levels_first = gather_levels(packed_first, lines)
    levels_first, packed_branch = tie(levels_first, packed_branch)
    levels_branch = gather_levels(packed_branch, lines)
    w_first, w_second = spread(levels_first, first_cut, lines)
    w_first, w_second, packed_up, levels_branch = tie(w_first, w_second, packed_up, levels_branch)
    levels_up = gather_levels(packed_up, lines)
    w_branch, w_down = spread(levels_branch, output_weight.shape[1], lines)
    w_gate, w_up = spread(levels_up, gate_weight.shape[1], lines)
    order_tokens = permutation((mixer_gate.shape[0],), lines)
    order_branch = permutation((mixer_output.shape[0], output_weight.shape[0]), lines)
    order_hidden = permutation((down_weight.shape[0],), lines)
    tokens = inputs[0].astype(jnp.float32)
    normed, norm_back = jax.vjp(rms_scale, tokens, input_gain)
    normed_low = normed.astype(jnp.bfloat16)
    normed_rel = to_relative(normed_low, order_tokens)
    first_out = product_rel(normed_rel, w_first)
    second_out = product_rel(normed_rel, w_second)
    gate_mix = first_out[:, :inner]
    queries = first_out[:, inner : inner + query_width]
    step_raw = first_out[:, inner + query_width : inner + query_width + SSM_HEADS]
    mixed_raw = second_out[:, :conv_width].astype(jnp.bfloat16)
    keys_raw = second_out[:, conv_width : conv_width + key_width]
    values_low = second_out[:, conv_width + key_width :].astype(jnp.bfloat16)
    rim_rows = passed_along(mixed_raw[local_len - CONV + 1 :], "seq", 1)
    extended = jnp.concatenate([rim_rows, mixed_raw], axis=0).astype(jnp.float32)

    def filter_fn(ext_rows, taps, bias):
        return conv_apply(ext_rows, ext_segments, taps, bias)

    filtered, filter_back = jax.vjp(filter_fn, extended, filter_taps, filter_bias)
    filtered_low = lax.optimization_barrier(filtered.astype(jnp.bfloat16)).astype(jnp.float32)

    def state_fn(xc_rows, step_in, bias, decay):
        return ssd_state(xc_rows, step_in, bias, decay, own_segments, seg_before)

    (carry_decay, carry_state), state_back = jax.vjp(
        state_fn, filtered_low, step_raw, step_bias, decay_log
    )
    state_rows = SSM_HEADS * SSM_HEAD
    packed_state = jnp.concatenate(
        [
            carry_state.reshape(state_rows, STATE),
            jnp.broadcast_to(carry_decay[:, None], (SSM_HEADS, STATE)),
        ]
    ).astype(jnp.bfloat16)
    earlier_states = [from_earlier(packed_state, d) for d in range(1, pieces)]
    later_decays = [
        from_earlier(packed_state[state_rows:, :1], -d)[:, 0].astype(jnp.float32)
        for d in range(1, pieces)
    ]
    start_state = jnp.zeros_like(carry_state)
    for d in range(pieces - 1, 0, -1):
        there = earlier_states[d - 1].astype(jnp.float32)
        start_state = (
            there[state_rows:, :1][:, :, None] * start_state
            + there[:state_rows].reshape(SSM_HEADS, SSM_HEAD, STATE)
        )
    incoming = (None, start_state)

    def output_fn(xc_rows, step_in, bias, decay, skip, start_state):
        return ssd_output(
            xc_rows, step_in, bias, decay, skip, own_segments, seg_before, start_state
        )

    ssm_out, output_back = jax.vjp(
        output_fn, filtered_low, step_raw, step_bias, decay_log, skip_gain, incoming[1]
    )
    gated_out, gated_back = jax.vjp(gated_norm, ssm_out, gate_mix, mixer_gain)
    gated_low = gated_out.astype(jnp.bfloat16)
    query_rot = rotate(queries.reshape(local_len, HEADS, HEAD), positions, 1.0).astype(jnp.bfloat16)
    key_rot = rotate(keys_raw.reshape(local_len, KV_HEADS, HEAD), positions, 1.0).astype(
        jnp.bfloat16
    )
    own_keys = jnp.concatenate([key_rot.reshape(local_len, key_width), values_low], axis=1)
    all_keys = jnp.concatenate(
        [own_keys] + [from_earlier(own_keys, d) for d in range(1, pieces)], axis=0
    )
    key_positions = jnp.concatenate([positions - d * local_len for d in range(pieces)])
    key_segments = jnp.concatenate(
        [
            lax.dynamic_slice_in_dim(all_segs, jnp.maximum(first_token - d * local_len, 0), local_len)
            for d in range(pieces)
        ]
    )
    allowed = (
        (key_positions[None, :] <= positions[:, None])
        & (key_positions >= 0)[None, :]
        & (key_segments[None, :] == own_segments[:, None])
    )
    repeat = HEADS // KV_HEADS

    def group_scores(group_index):
        query_group = query_rot[:, group_index * repeat : (group_index + 1) * repeat]
        key_group = all_keys[:, group_index * HEAD : (group_index + 1) * HEAD]
        value_group = all_keys[:, key_width + group_index * HEAD : key_width + (group_index + 1) * HEAD]
        scores = (
            jnp.einsum("prd,kd->rpk", query_group, key_group, preferred_element_type=jnp.float32)
            * score_scale
        )
        return (query_group, key_group, value_group, jnp.where(allowed[None], scores, -1e30))

    group_lse = []
    group_out = []
    group_exact = []
    for group_index in range(KV_HEADS):
        query_group, key_group, value_group, scores = group_scores(group_index)
        top = jnp.max(scores, axis=-1)
        lse_group = top + jnp.log(jnp.sum(jnp.exp(scores - top[..., None]), axis=-1))
        probs = jnp.exp(scores - lse_group[..., None])
        group_out.append(
            jnp.einsum(
                "rpk,kd->prd",
                probs.astype(jnp.bfloat16),
                value_group,
                preferred_element_type=jnp.float32,
            )
        )
        group_exact.append(
            jnp.einsum(
                "rpk,kd->prd",
                probs,
                value_group.astype(jnp.float32),
                preferred_element_type=jnp.float32,
            )
        )
        group_lse.append(lse_group)
    attended = jnp.concatenate(group_out, axis=1)
    attended_low = attended.reshape(local_len, HEADS * HEAD).astype(jnp.bfloat16)
    branch_rel = to_relative(jnp.concatenate([gated_low, attended_low], axis=1), order_branch)
    middle = tokens + product_rel(branch_rel, w_branch)
    second, second_back = jax.vjp(rms_scale, middle, second_gain)
    second_low = second.astype(jnp.bfloat16)
    second_rel = to_relative(second_low, order_tokens)
    gate_val = product_rel(second_rel, w_gate)
    up_val = product_rel(second_rel, w_up)
    activated, act_back = jax.vjp(swiglu, gate_val, up_val)
    activated_low = activated.astype(jnp.bfloat16)
    activated_rel = to_relative(activated_low, order_hidden)
    result = (middle + product_rel(activated_rel, w_down)).astype(jnp.bfloat16)
    upstream = cotangent[0].astype(jnp.float32)
    upstream_low = upstream.astype(jnp.bfloat16)
    grad_act = from_relative(back_rel(upstream_low, w_down), order_hidden)
    grad_gate_val, grad_up_val = act_back(grad_act)
    gate_grad_low = grad_gate_val.astype(jnp.bfloat16)
    up_grad_low = grad_up_val.astype(jnp.bfloat16)
    sum_up = owed([(second_rel, gate_grad_low), (second_rel, up_grad_low)], lines)
    up_wait = next(sum_up)
    grad_second = from_relative(
        back_rel(gate_grad_low, w_gate) + back_rel(up_grad_low, w_up), order_tokens
    )
    grad_middle, grad_second_gain = second_back(grad_second)
    grad_middle = grad_middle + upstream
    grad_middle, up_wait = tie(grad_middle, up_wait)
    up_wait = sum_up.send(up_wait)
    branch_low = grad_middle.astype(jnp.bfloat16)
    sum_branch = owed([(activated_rel, upstream_low), (branch_rel, branch_low)], lines)
    branch_wait = next(sum_branch)
    grad_branch = from_relative(back_rel(branch_low, w_branch), order_branch)
    grad_gated = grad_branch[:, :inner]
    grad_attn = grad_branch[:, inner:].astype(jnp.bfloat16).reshape(local_len, HEADS, HEAD)
    grad_ssm, grad_zgate, grad_mixer_gain = gated_back(grad_gated)
    zgate_low = grad_zgate.astype(jnp.bfloat16)
    grad_ssm, zgate_low, branch_wait, up_wait = tie(grad_ssm, zgate_low, branch_wait, up_wait)
    branch_wait = sum_branch.send(branch_wait)
    up_wait = sum_up.send(up_wait)
    query_grads = []
    key_grads = []
    value_grads = []
    for group_index in range(KV_HEADS):
        query_group, key_group, value_group, scores = group_scores(group_index)
        grad_group = grad_attn[:, group_index * repeat : (group_index + 1) * repeat]
        lse_group = group_lse[group_index]
        row_delta = jnp.einsum(
            "prd,prd->rp", grad_group.astype(jnp.float32), group_exact[group_index]
        )
        probs = jnp.exp(scores - lse_group[..., None])
        value_grads.append(
            jnp.einsum(
                "rpk,prd->kd",
                probs.astype(jnp.bfloat16),
                grad_group,
                preferred_element_type=jnp.float32,
            )
        )
        grad_probs = jnp.einsum(
            "prd,kd->rpk", grad_group, value_group, preferred_element_type=jnp.float32
        )
        grad_scores = (probs * (grad_probs - row_delta[..., None])).astype(jnp.bfloat16)
        query_grads.append(
            score_scale
            * jnp.einsum("rpk,kd->prd", grad_scores, key_group, preferred_element_type=jnp.float32)
        )
        key_grads.append(
            score_scale
            * jnp.einsum("rpk,prd->kd", grad_scores, query_group, preferred_element_type=jnp.float32)
        )
    keys_part = jnp.concatenate(key_grads + value_grads, axis=1)
    keys_total = keys_part[:local_len]
    for d in range(1, pieces):
        sent = keys_part[d * local_len : (d + 1) * local_len].astype(jnp.bfloat16)
        keys_total = keys_total + from_earlier(sent, -d).astype(jnp.float32)
    key_total = keys_total[:, :key_width]
    value_total = keys_total[:, key_width:]
    query_low = (
        rotate(jnp.concatenate(query_grads, axis=1), positions, -1.0)
        .reshape(local_len, HEADS * HEAD)
        .astype(jnp.bfloat16)
    )
    key_low = (
        rotate(key_total.reshape(local_len, KV_HEADS, HEAD), positions, -1.0)
        .reshape(local_len, KV_HEADS * HEAD)
        .astype(jnp.bfloat16)
    )
    value_low = value_total.astype(jnp.bfloat16)
    head_low = jnp.concatenate([query_low, key_low, value_low], axis=1)
    sum_heads = owed([(normed_rel, zgate_low), (normed_rel, head_low)], lines)
    grad_ssm, query_low, branch_wait, up_wait = tie(grad_ssm, query_low, branch_wait, up_wait)
    branch_wait = sum_branch.send(branch_wait)
    up_wait = sum_up.send(up_wait)
    xc_first, step_first, bias_first, decay_first, grad_skip, grad_incoming = output_back(grad_ssm)
    heads_wait = next(sum_heads)
    grad_incoming, branch_wait, up_wait = tie(grad_incoming, branch_wait, up_wait)
    branch_wait = sum_branch.send(branch_wait)
    grad_gate, grad_up = sum_up.send(up_wait)
    packed_grad = grad_incoming.astype(jnp.bfloat16)
    carried = jnp.zeros_like(grad_incoming)
    for d in range(pieces - 1, 0, -1):
        there = from_earlier(packed_grad, -d).astype(jnp.float32)
        carried = later_decays[d - 1][:, None, None] * carried + there
    grad_decay_total = jnp.sum(carried * incoming[1], axis=(1, 2))
    xc_second, step_second, bias_second, decay_second = state_back((grad_decay_total, carried))
    xc_second, branch_wait, heads_wait = tie(xc_second, branch_wait, heads_wait)
    grad_down, grad_branch_rows = sum_branch.send(branch_wait)
    heads_wait = sum_heads.send(heads_wait)
    grad_ext, grad_taps, grad_fbias = filter_back(xc_first + xc_second)
    returned = passed_along(grad_ext[: CONV - 1], "seq", -1)
    grad_mixed = grad_ext[CONV - 1 :] + jnp.pad(returned, ((local_len - CONV + 1, 0), (0, 0)))
    mixed_grad_low = grad_mixed.astype(jnp.bfloat16)
    step_grad_low = (step_first + step_second).astype(jnp.bfloat16)
    mixed_grad_low, heads_wait = tie(mixed_grad_low, heads_wait)
    heads_wait = sum_heads.send(heads_wait)
    step_pad_low = jnp.pad(step_grad_low, ((0, 0), (0, 128 - SSM_HEADS)))
    cut = (conv_width + 128) // 256 * 128
    mixed_first = mixed_grad_low[:, :cut]
    mixed_rest = jnp.concatenate([mixed_grad_low[:, cut:], step_pad_low], axis=1)
    sum_mixed = owed([(normed_rel, mixed_first), (normed_rel, mixed_rest)], lines)
    mixed_wait = next(sum_mixed)
    mixed_wait = sum_mixed.send(mixed_wait)
    mixed_wait, heads_wait = tie(mixed_wait, heads_wait)
    heads_wait = sum_heads.send(heads_wait)
    grad_mixer_gate, grad_heads = sum_heads.send(heads_wait)
    mixed_wait = sum_mixed.send(mixed_wait)
    mixed_wait = sum_mixed.send(mixed_wait)
    grad_mixed_first, grad_mixed_rest = sum_mixed.send(mixed_wait)
    first_low = jnp.concatenate([zgate_low, query_low, step_pad_low], axis=1)
    second_grad_low = jnp.concatenate([mixed_grad_low, key_low, value_low], axis=1)
    grad_normed = from_relative(
        back_rel(first_low, w_first) + back_rel(second_grad_low, w_second), order_tokens
    )
    rest_width = conv_width - cut
    mixer_rows = mixer_output.shape[0]
    mixer_grads = (
        grad_mixer_gate,
        jnp.concatenate([grad_mixed_first, grad_mixed_rest[:, :rest_width]], axis=1),
        grad_mixed_rest[:, rest_width : rest_width + SSM_HEADS],
        grad_branch_rows[:mixer_rows],
        grad_heads[:, :query_width],
        grad_heads[:, query_width : query_width + key_width],
        grad_heads[:, query_width + key_width :],
        grad_branch_rows[mixer_rows:],
    )
    ffn_grads = (grad_gate, grad_up, grad_down)
    grad_tokens, grad_input_gain = norm_back(grad_normed)
    grad_tokens = grad_tokens + grad_middle
    small = (
        grad_input_gain,
        grad_second_gain,
        grad_mixer_gain,
        grad_taps,
        grad_fbias,
        decay_first + decay_second,
        bias_first + bias_second,
        grad_skip,
    )
    sizes = [part.size for part in small]
    length = sum(sizes)
    flat = jnp.pad(
        jnp.concatenate([part.reshape(-1) for part in small]), (0, -length % 1024)
    ).reshape(-1, 128)
    flat = sum_everywhere(flat).reshape(-1)
    small_sums = []
    start = 0
    for part in small:
        small_sums.append(flat[start : start + part.size].reshape(part.shape))
        start += part.size
    return (
        result[None],
        grad_tokens[None],
        mixer_grads[0],
        mixer_grads[1],
        mixer_grads[2],
        mixer_grads[3],
        mixer_grads[4],
        mixer_grads[5],
        mixer_grads[6],
        mixer_grads[7],
        ffn_grads[0],
        ffn_grads[1],
        ffn_grads[2],
        small_sums[0],
        small_sums[1],
        small_sums[2],
        small_sums[3],
        small_sums[4],
        small_sums[5],
        small_sums[6],
        small_sums[7],
    )


def solution(mesh):
    placed = (
        P("dp", "seq", None),
        P("dp", None),
        P("dp", "seq", None),
        P(("dp", "seq"), None),
        P(("dp", "seq"), None),
        P(("dp", "seq"), None),
        P(("dp", "seq"), None),
        P(("dp", "seq"), None),
        P(("dp", "seq"), None),
        P(("dp", "seq"), None),
        P(("dp", "seq"), None),
        P(("dp", "seq"), None),
        P(("dp", "seq"), None),
        P(("dp", "seq"), None),
        P(),
        P(),
        P(),
        P(),
        P(),
        P(),
        P(),
        P(),
    )
    return jax.shard_map(
        body,
        mesh=mesh,
        in_specs=placed,
        out_specs=(
            P("dp", "seq", None),
            P("dp", "seq", None),
            P(("dp", "seq"), None),
            P(("dp", "seq"), None),
            P(("dp", "seq"), None),
            P(("dp", "seq"), None),
            P(("dp", "seq"), None),
            P(("dp", "seq"), None),
            P(("dp", "seq"), None),
            P(("dp", "seq"), None),
            P(("dp", "seq"), None),
            P(("dp", "seq"), None),
            P(("dp", "seq"), None),
            P(),
            P(),
            P(),
            P(),
            P(),
            P(),
            P(),
            P(),
        ),
        check_vma=False,
    )
```

```python
import functools

import jax
import jax.numpy as jnp
from jax import lax
from jax.experimental import pallas as pl
from jax.experimental.pallas import tpu as pltpu
from jax.sharding import PartitionSpec as P

HEADS = 8
KV_HEADS = 2
HEAD = 64
SSM_HEADS = 24
SSM_HEAD = 64
STATE = 128
CONV = 4


eps = 1e-05
rope_theta = 100000000000.0
score_scale = 0.125


def passed_along(x, axis, by):
    length = lax.axis_size(axis)
    pairs = [(i, i + by) for i in range(length) if 0 <= i + by < length]
    return lax.ppermute(x, axis, pairs)


def matmul(left, right):
    return jnp.dot(left, right, preferred_element_type=jnp.float32)


def rows_product(left, right):
    return lax.dot_general(
        left, right, (((0,), (0,)), ((), ())), preferred_element_type=jnp.float32
    )


def back_product(left, right):
    return lax.dot_general(
        left, right, (((1,), (1,)), ((), ())), preferred_element_type=jnp.float32
    )


def rms_scale(tensor, scale_gain):
    return tensor * lax.rsqrt(jnp.mean(tensor * tensor, axis=-1, keepdims=True) + eps) * scale_gain


def rotation_tables(positions):
    half_width = HEAD // 2
    frequency = rope_theta ** (-jnp.arange(half_width, dtype=jnp.float32) / half_width)
    angle = positions.astype(jnp.float32)[:, None] * frequency[None, :]
    cosine = jnp.cos(angle)
    sine = jnp.sin(angle)
    return (
        jnp.concatenate([cosine] * 4, axis=1),
        jnp.concatenate([-sine, sine, -sine, sine], axis=1),
    )


def conv_apply(extended, ext_segments, filter_taps, filter_bias):
    length = extended.shape[0] - CONV + 1
    own_segment = ext_segments[CONV - 1 :]
    summed = jnp.zeros((length, extended.shape[1]), jnp.float32) + filter_bias[None, :]
    for offset in range(CONV):
        match_mask = (ext_segments[offset : offset + length] == own_segment).astype(jnp.float32)[
            :, None
        ]
        summed = (
            summed + filter_taps[offset][None, :] * extended[offset : offset + length] * match_mask
        )
    return jax.nn.silu(summed)


def running_sum(x):
    order = jnp.arange(x.shape[0])
    earlier = (order[:, None] >= order[None, :]).astype(jnp.float32)
    return jnp.dot(earlier, x, precision=lax.Precision.HIGHEST)


def later_sum(x):
    order = jnp.arange(x.shape[0])
    later = (order[:, None] <= order[None, :]).astype(jnp.float32)
    return jnp.dot(later, x, precision=lax.Precision.HIGHEST)


PAIR = 128
DECAY_ROWS = 32


def dot_nn(left, right):
    return jnp.dot(left, right, preferred_element_type=jnp.float32)


def dot_nt(left, right):
    return lax.dot_general(
        left, right, (((1,), (1,)), ((), ())), preferred_element_type=jnp.float32
    )


def dot_tn(left, right):
    return lax.dot_general(
        left, right, (((0,), (0,)), ((), ())), preferred_element_type=jnp.float32
    )


def low(x):
    return x.astype(jnp.bfloat16)


def lane_index(shape):
    return lax.broadcasted_iota(jnp.int32, shape, 1)


def column_of(table, index):
    return jnp.sum(jnp.where(lane_index(table.shape) == index, table, 0.0), axis=1, keepdims=True)


def set_column(ref, index, column):
    table = ref[...]
    ref[...] = jnp.where(lane_index(table.shape) == index, column, table)


def by_head(first, second, shape):
    return jnp.where(lane_index(shape) < HEAD, first, second)


def whole_spec(shape):
    return pl.BlockSpec(shape, lambda i: (0,) * len(shape))


def pair_spec(rows):
    return pl.BlockSpec((rows, PAIR), lambda i: (0, i))


def state_spec():
    return pl.BlockSpec((PAIR, STATE), lambda i: (i, 0))


def call(kernel, grid, in_specs, out_specs, out_shape, scratch=(), flops=0):
    return pl.pallas_call(
        kernel,
        grid=(grid,),
        in_specs=in_specs,
        out_specs=out_specs,
        out_shape=out_shape,
        scratch_shapes=list(scratch),
        compiler_params=pltpu.CompilerParams(
            dimension_semantics=("arbitrary",), vmem_limit_bytes=40 * 1024 * 1024
        ),
        cost_estimate=pl.CostEstimate(flops=flops, bytes_accessed=4000000, transcendentals=0),
    )


def float_out(*shape):
    return jax.ShapeDtypeStruct(shape, jnp.float32)


def masked_products(read_ref, write_ref, seg_col, seg_row):
    products = dot_nt(read_ref[...], write_ref[...])
    row = lax.broadcasted_iota(jnp.int32, products.shape, 0)
    allowed = (row >= lane_index(products.shape)) & (seg_col[...] == seg_row[...])
    return jnp.where(allowed, products, 0.0)


def ssd_local_kernel(
    value_ref, write_ref, read_ref, run_ref, run_row, stride_row, end_ref, skip_ref, seg_col,
    seg_row, out_ref, state_ref, products,
):
    step = pl.program_id(0)

    @pl.when(step == 0)
    def _():
        products[...] = masked_products(read_ref, write_ref, seg_col, seg_row)

    value = value_ref[...]
    wide = value.astype(jnp.float32)
    outs = []
    for half in range(2):
        head = 2 * step + half
        gap = column_of(run_ref[...], head) - run_row[pl.ds(head, 1), :]
        mixing = jnp.exp(jnp.minimum(gap, 0.0)) * products[...] * stride_row[pl.ds(head, 1), :]
        outs.append(dot_nn(low(mixing), value))
    skip = by_head(
        column_of(skip_ref[...], 2 * step), column_of(skip_ref[...], 2 * step + 1), (1, PAIR)
    )
    out_ref[...] = by_head(outs[0], outs[1], wide.shape) + skip * wide
    weight = by_head(
        column_of(end_ref[...], 2 * step), column_of(end_ref[...], 2 * step + 1), wide.shape
    )
    state_ref[...] = dot_tn(low(weight * wide), write_ref[...])


def ssd_local(filtered, running, run_rows, stride_rows, end_weights, skip_gain, seg_col, seg_row):
    length = filtered.shape[0]
    pairs = SSM_HEADS // 2
    inner = SSM_HEADS * SSM_HEAD
    return call(
        ssd_local_kernel,
        pairs,
        [
            pair_spec(length),
            pl.BlockSpec((length, STATE), lambda i: (0, pairs)),
            pl.BlockSpec((length, STATE), lambda i: (0, pairs + 1)),
            whole_spec((length, SSM_HEADS)),
            whole_spec((SSM_HEADS, length)),
            whole_spec((SSM_HEADS, length)),
            whole_spec((length, SSM_HEADS)),
            whole_spec((1, SSM_HEADS)),
            whole_spec((length, 1)),
            whole_spec((1, length)),
        ],
        [pair_spec(length), state_spec()],
        [float_out(length, inner), float_out(inner, STATE)],
        [pltpu.VMEM((length, length), jnp.float32)],
        2 * SSM_HEADS * length * length * PAIR,
    )(
        filtered, filtered, filtered, running, run_rows, stride_rows, end_weights,
        skip_gain[None, :], seg_col, seg_row,
    )


def chained(message_refs, step):
    first = (lax.broadcasted_iota(jnp.int32, (PAIR, STATE), 0) // SSM_HEAD) == 0
    state = jnp.zeros((PAIR, STATE), jnp.float32)
    for block_ref, decay_ref in reversed(message_refs):
        decays = decay_ref[...].astype(jnp.float32)
        row = lax.broadcasted_iota(jnp.int32, decays.shape, 0)
        one = jnp.sum(jnp.where(row == 2 * step, decays, 0.0), axis=0, keepdims=True)
        two = jnp.sum(jnp.where(row == 2 * step + 1, decays, 0.0), axis=0, keepdims=True)
        state = jnp.where(first, one, two) * state + block_ref[...].astype(jnp.float32)
    return state


def message_specs(count):
    blocks = SSM_HEADS * SSM_HEAD // DECAY_ROWS
    return [
        spec
        for _ in range(count)
        for spec in (state_spec(), pl.BlockSpec((DECAY_ROWS, STATE), lambda i: (blocks, 0)))
    ]


def packed_message(states, decays):
    rows = jnp.broadcast_to(jnp.pad(decays, (0, DECAY_ROWS - SSM_HEADS))[:, None], (DECAY_ROWS, STATE))
    return jnp.concatenate([low(states), low(rows)])


def ssd_entering_kernel(local_ref, read_ref, enter_ref, *refs):
    message_refs, (out_ref, state_ref) = (refs[:-2], refs[-2:])
    step = pl.program_id(0)
    shape = local_ref.shape
    state_ref[...] = chained(list(zip(message_refs[::2], message_refs[1::2])), step)
    enter = by_head(
        column_of(enter_ref[...], 2 * step), column_of(enter_ref[...], 2 * step + 1), shape
    )
    out_ref[...] = local_ref[...] + enter * dot_nt(read_ref[...], low(state_ref[...]))


def ssd_entering(local, filtered, entering, messages):
    length = filtered.shape[0]
    pairs = SSM_HEADS // 2
    inner = SSM_HEADS * SSM_HEAD
    return call(
        ssd_entering_kernel,
        pairs,
        [
            pair_spec(length),
            pl.BlockSpec((length, STATE), lambda i: (0, pairs + 1)),
            whole_spec((length, SSM_HEADS)),
        ]
        + message_specs(len(messages)),
        [pair_spec(length), state_spec()],
        [float_out(*local.shape), float_out(inner, STATE)],
        (),
        2 * SSM_HEADS * length * STATE * SSM_HEAD,
    )(local, filtered, entering, *[m for message in messages for m in (message, message)])


def ssd_back_kernel(
    grad_ref, value_ref, write_ref, read_ref, run_ref, run_row, stride_row, enter_ref, skip_ref,
    state_ref, seg_col, seg_row, value_grad, state_grad, row_sum, col_sum, write_grad, read_grad,
    products, total,
):
    step = pl.program_id(0)

    @pl.when(step == 0)
    def _():
        products[...] = masked_products(read_ref, write_ref, seg_col, seg_row)
        total[...] = jnp.zeros_like(total)
        row_sum[...] = jnp.zeros_like(row_sum)
        read_grad[...] = jnp.zeros_like(read_grad)

    value = value_ref[...]
    grad = grad_ref[...]
    shape = grad.shape
    skip = by_head(
        column_of(skip_ref[...], 2 * step), column_of(skip_ref[...], 2 * step + 1), (1, PAIR)
    )
    enter = by_head(
        column_of(enter_ref[...], 2 * step), column_of(enter_ref[...], 2 * step + 1), shape
    )
    state = low(state_ref[...])
    read = read_ref[...]
    entered = enter * grad
    from_state = entered * dot_nt(read, state)
    entered = low(entered)
    state_grad[...] = dot_tn(entered, read)
    read_grad[...] += dot_nn(entered, state)
    into_values = skip * grad
    for half in range(2):
        head = 2 * step + half
        inside = (lane_index(shape) // HEAD) == half
        part = low(jnp.where(inside, grad, 0.0))
        gap = column_of(run_ref[...], head) - run_row[pl.ds(head, 1), :]
        decay = jnp.exp(jnp.minimum(gap, 0.0))
        strides = stride_row[pl.ds(head, 1), :]
        weighted = dot_nt(part, value) * decay
        total[...] += weighted * strides
        scaled = weighted * products[...]
        col_sum[pl.ds(head, 1), :] = jnp.sum(scaled, axis=0, keepdims=True)
        rows = jnp.sum(scaled * strides, axis=1, keepdims=True) + jnp.sum(
            jnp.where(inside, from_state, 0.0), axis=1, keepdims=True
        )
        set_column(row_sum, head, rows)
        mixing = decay * products[...] * strides
        into_values = into_values + dot_tn(low(mixing), part)
    value_grad[...] = into_values

    @pl.when(step == pl.num_programs(0) - 1)
    def _():
        sums = total[...]
        row = lax.broadcasted_iota(jnp.int32, sums.shape, 0)
        allowed = (row >= lane_index(sums.shape)) & (seg_col[...] == seg_row[...])
        sums = low(jnp.where(allowed, sums, 0.0))
        write_grad[...] = dot_tn(sums, read)
        read_grad[...] += dot_nn(sums, write_ref[...])


def ssd_back(
    grad, filtered, running, run_rows, stride_rows, entering, skip_gain, state, seg_col, seg_row
):
    length = filtered.shape[0]
    pairs = SSM_HEADS // 2
    inner = SSM_HEADS * SSM_HEAD
    return call(
        ssd_back_kernel,
        pairs,
        [
            pair_spec(length),
            pair_spec(length),
            pl.BlockSpec((length, STATE), lambda i: (0, pairs)),
            pl.BlockSpec((length, STATE), lambda i: (0, pairs + 1)),
            whole_spec((length, SSM_HEADS)),
            whole_spec((SSM_HEADS, length)),
            whole_spec((SSM_HEADS, length)),
            whole_spec((length, SSM_HEADS)),
            whole_spec((1, SSM_HEADS)),
            state_spec(),
            whole_spec((length, 1)),
            whole_spec((1, length)),
        ],
        [
            pair_spec(length),
            state_spec(),
            whole_spec((length, SSM_HEADS)),
            whole_spec((SSM_HEADS, length)),
            whole_spec((length, STATE)),
            whole_spec((length, STATE)),
        ],
        [
            float_out(length, inner),
            float_out(inner, STATE),
            float_out(length, SSM_HEADS),
            float_out(SSM_HEADS, length),
            float_out(length, STATE),
            float_out(length, STATE),
        ],
        [pltpu.VMEM((length, length), jnp.float32), pltpu.VMEM((length, length), jnp.float32)],
        4 * SSM_HEADS * length * length * PAIR,
    )(
        grad, filtered, filtered, filtered, running, run_rows, stride_rows, entering,
        skip_gain[None, :], state, seg_col, seg_row,
    )


def ssd_state_back_kernel(
    value_ref, write_ref, end_ref, before_ref, write_before, start_ref, *refs
):
    message_refs, (value_grad, end_grad, write_grad, decay_grad) = (refs[:-4], refs[-4:])
    step = pl.program_id(0)

    @pl.when(step == 0)
    def _():
        end_grad[...] = jnp.zeros_like(end_grad)
        write_grad[...] = write_before[...]
        decay_grad[...] = jnp.zeros_like(decay_grad)

    wide = value_ref[...].astype(jnp.float32)
    shape = wide.shape
    weight = by_head(
        column_of(end_ref[...], 2 * step), column_of(end_ref[...], 2 * step + 1), shape
    )
    carried = chained(list(zip(message_refs[::2], message_refs[1::2])), step)
    products = jnp.sum(carried * start_ref[...], axis=1, keepdims=True)
    first = lax.broadcasted_iota(jnp.int32, products.shape, 0) // SSM_HEAD == 0
    head = lane_index(decay_grad.shape)
    for half in range(2):
        total = jnp.sum(jnp.where(first == (half == 0), products, 0.0), axis=0, keepdims=True)
        decay_grad[...] = jnp.where(head == 2 * step + half, total, decay_grad[...])
    carried = low(carried)
    reached = dot_nt(write_ref[...], carried)
    value_grad[...] = before_ref[...] + weight * reached
    write_grad[...] += dot_nn(low(weight * wide), carried)
    product = wide * reached
    for half in range(2):
        inside = (lane_index(shape) // HEAD) == half
        set_column(
            end_grad,
            2 * step + half,
            jnp.sum(jnp.where(inside, product, 0.0), axis=1, keepdims=True),
        )


def ssd_state_back(filtered, end_weights, value_before, write_before, start, messages):
    length = filtered.shape[0]
    pairs = SSM_HEADS // 2
    return call(
        ssd_state_back_kernel,
        pairs,
        [
            pair_spec(length),
            pl.BlockSpec((length, STATE), lambda i: (0, pairs)),
            whole_spec((length, SSM_HEADS)),
            pair_spec(length),
            whole_spec((length, STATE)),
            state_spec(),
        ]
        + message_specs(len(messages)),
        [
            pair_spec(length),
            whole_spec((length, SSM_HEADS)),
            whole_spec((length, STATE)),
            whole_spec((1, SSM_HEADS)),
        ],
        [
            float_out(*value_before.shape),
            float_out(length, SSM_HEADS),
            float_out(length, STATE),
            float_out(1, SSM_HEADS),
        ],
        (),
        4 * SSM_HEADS * length * STATE * SSM_HEAD,
    )(
        filtered, filtered, end_weights, value_before, write_before, start,
        *[m for message in messages for m in (message, message)],
    )


def turned(x, cosine, sine):
    quarter = HEAD // 2
    after = pltpu.roll(x, x.shape[1] - quarter, 1)
    earlier = pltpu.roll(x, quarter, 1)
    other = jnp.where(lane_index(x.shape) % HEAD < quarter, after, earlier)
    return x * cosine + other * sine


def group_rows(both, group):
    wide = both.astype(jnp.float32)
    kept = jnp.where(lane_index(wide.shape) // HEAD == group, wide, 0.0)
    return low(kept + pltpu.roll(kept, HEAD, 1))


def attention_mask(bias, pos_col, pos_row, seg_col, seg_row):
    allowed = (
        (pos_row[...] <= pos_col[...]) & (pos_row[...] >= 0) & (seg_row[...] == seg_col[...])
    )
    bias[...] = jnp.where(allowed, 0.0, -1e30)


def attention_kernel(
    query_ref, keys_ref, values_ref, cos_ref, sin_ref, pos_col, pos_row, seg_col, seg_row, out_ref,
    lse_ref, bias,
):
    step = pl.program_id(0)

    @pl.when(step == 0)
    def _():
        attention_mask(bias, pos_col, pos_row, seg_col, seg_row)
        lse_ref[...] = jnp.zeros_like(lse_ref)

    group = step * 2 // (HEADS // KV_HEADS)
    keys = group_rows(keys_ref[...], group)
    values = group_rows(values_ref[...], group)
    query = low(turned(query_ref[...], cos_ref[...], sin_ref[...])).astype(jnp.float32)
    outs = []
    for half in range(2):
        inside = (lane_index(query.shape) // HEAD) == half
        part = low(jnp.where(inside, query, 0.0))
        scores = dot_nt(part, keys) * score_scale + bias[...]
        top = jnp.max(scores, axis=1, keepdims=True)
        lse = top + jnp.log(jnp.sum(jnp.exp(scores - top), axis=1, keepdims=True))
        outs.append(dot_nn(low(jnp.exp(scores - lse)), values))
        set_column(lse_ref, 2 * step + half, lse)
    out_ref[...] = low(by_head(outs[0], outs[1], query.shape))


def attention_specs(length, keys):
    return [
        whole_spec((length, PAIR)),
        whole_spec((length, PAIR)),
        whole_spec((length, 1)),
        whole_spec((1, keys)),
        whole_spec((length, 1)),
        whole_spec((1, keys)),
    ]


def attention(queries, all_keys, places):
    length = queries.shape[0]
    keys = all_keys.shape[0]
    return call(
        attention_kernel,
        HEADS // 2,
        [
            pair_spec(length),
            pl.BlockSpec((keys, PAIR), lambda i: (0, 0)),
            pl.BlockSpec((keys, PAIR), lambda i: (0, 1)),
        ]
        + attention_specs(length, keys),
        [pair_spec(length), whole_spec((length, HEADS))],
        [jax.ShapeDtypeStruct(queries.shape, jnp.bfloat16), float_out(length, HEADS)],
        [pltpu.VMEM((length, keys), jnp.float32)],
        4 * HEADS * length * keys * PAIR,
    )(queries, all_keys, all_keys, *places)


def attention_back_kernel(
    query_ref, grad_ref, lse_ref, keys_ref, values_ref, cos_ref, sin_ref, pos_col, pos_row,
    seg_col, seg_row, query_grad, key_grad, value_grad, bias,
):
    step = pl.program_id(0)

    @pl.when(step == 0)
    def _():
        attention_mask(bias, pos_col, pos_row, seg_col, seg_row)
        key_grad[...] = jnp.zeros_like(key_grad)
        value_grad[...] = jnp.zeros_like(value_grad)

    group = step * 2 // (HEADS // KV_HEADS)
    keys = group_rows(keys_ref[...], group)
    values = group_rows(values_ref[...], group)
    query = low(turned(query_ref[...], cos_ref[...], sin_ref[...])).astype(jnp.float32)
    grad = low(grad_ref[...]).astype(jnp.float32)
    into_query = []
    into_keys = jnp.zeros(key_grad.shape, jnp.float32)
    into_values = jnp.zeros(key_grad.shape, jnp.float32)
    for half in range(2):
        inside = (lane_index(query.shape) // HEAD) == half
        part = low(jnp.where(inside, query, 0.0))
        grad_part = low(jnp.where(inside, grad, 0.0))
        scores = dot_nt(part, keys) * score_scale + bias[...]
        probs = jnp.exp(scores - column_of(lse_ref[...], 2 * step + half))
        grad_probs = dot_nt(grad_part, values)
        delta = jnp.sum(probs * grad_probs, axis=1, keepdims=True)
        grad_scores = low(probs * (grad_probs - delta))
        into_query.append(dot_nn(grad_scores, keys))
        into_keys = into_keys + dot_tn(grad_scores, part)
        into_values = into_values + dot_tn(low(probs), grad_part)
    wide = by_head(into_query[0], into_query[1], query.shape) * score_scale
    query_grad[...] = low(turned(wide, cos_ref[...], -sin_ref[...]))
    mine = lane_index(into_keys.shape) // HEAD == group
    into_keys = into_keys + pltpu.roll(into_keys, HEAD, 1)
    into_values = into_values + pltpu.roll(into_values, HEAD, 1)
    key_grad[...] += jnp.where(mine, into_keys * score_scale, 0.0)
    value_grad[...] += jnp.where(mine, into_values, 0.0)


def attention_back(queries, grads, lse, all_keys, places):
    length = queries.shape[0]
    keys = all_keys.shape[0]
    return call(
        attention_back_kernel,
        HEADS // 2,
        [
            pair_spec(length),
            pair_spec(length),
            whole_spec((length, HEADS)),
            pl.BlockSpec((keys, PAIR), lambda i: (0, 0)),
            pl.BlockSpec((keys, PAIR), lambda i: (0, 1)),
        ]
        + attention_specs(length, keys),
        [pair_spec(length), whole_spec((keys, PAIR)), whole_spec((keys, PAIR))],
        [
            jax.ShapeDtypeStruct(queries.shape, jnp.bfloat16),
            float_out(keys, PAIR),
            float_out(keys, PAIR),
        ],
        [pltpu.VMEM((length, keys), jnp.float32)],
        10 * HEADS * length * keys * PAIR,
    )(queries, grads, lse, all_keys, all_keys, *places)


def turn_pair(x, cosine, sine):
    quarter = HEAD // 2
    pieces = [x[:, k * quarter : (k + 1) * quarter] for k in range(x.shape[1] // quarter)]
    other = jnp.concatenate([pieces[k ^ 1] for k in range(len(pieces))], axis=1)
    return x * cosine + other * sine


def gated_norm(ssm_out, gate_mix, mixer_gain):
    return rms_scale(ssm_out * jax.nn.silu(gate_mix), mixer_gain)


def swiglu(gate_val, up_val):
    return jax.nn.silu(gate_val) * up_val


def shift_along(x, line, by):
    axis, stride, size = line
    pairs = []
    for index in range(lax.axis_size(axis)):
        place = (index // stride) % size
        pairs.append((index, index + ((place + by) % size - place) * stride))
    return lax.ppermute(x, axis, pairs)


def mesh_lines():
    replicas, pieces = (lax.axis_size("dp"), lax.axis_size("seq"))
    across = 1
    while across * across * 2 <= pieces:
        across *= 2
    lines = {
        "core": ("dp", 1, 2),
        "z": ("dp", 2, replicas // 2),
        "x": ("seq", 1, across),
        "y": ("seq", across, pieces // across),
    }
    return lines


def place_on(line):
    axis, stride, size = line
    return (lax.axis_index(axis) // stride) % size


def tie(*groups):
    return lax.optimization_barrier(groups)


def shift_piece(x, lines, down, right):
    rows, across = (lines["y"][2], lines["x"][2])
    pairs = []
    for index in range(rows * across):
        y, x_place = (index // across, index % across)
        pairs.append((index, (y + down) % rows * across + (x_place + right) % across))
    return lax.ppermute(x, "seq", pairs)


def offsets(lines):
    return [(y, x) for y in range(lines["y"][2]) for x in range(lines["x"][2])]


def level_groups(line):
    axis, stride, size = line
    return [[c + stride * k for k in range(size)] for c in range(stride)]


def gather_levels(packed, lines):
    return lax.all_gather(packed, "dp")


def spread(both, widths, lines):
    levels, rows, width = (lines["z"][2], both.shape[1], both.shape[2])
    mine = lax.dynamic_index_in_dim(
        both.reshape(levels, 2, rows, width), place_on(lines["core"]), 1, False
    ).reshape(levels * rows, width)
    blocks = [shift_piece(mine, lines, -y, -x) if y or x else mine for y, x in offsets(lines)]
    found = []
    start = 0
    for size in widths:
        own = jnp.concatenate([block[:, start : start + size] for block in blocks], axis=0)
        found.append((own, shift_along(own, lines["core"], 1)))
        start += size
    return found


def relative_index(row_counts, lines):
    levels, rows_out, across = (lines["z"][2], lines["y"][2], lines["x"][2])
    total = sum(row_counts)
    places = []
    start = 0
    for rows in row_counts:
        column = jnp.arange(levels * 2 * rows_out * across * rows)
        row = column % rows
        device = column // rows
        x = (device % across - place_on(lines["x"])) % across
        y = (device // across % rows_out - place_on(lines["y"])) % rows_out
        core = (device // (across * rows_out) - place_on(lines["core"])) % 2
        level = device // (across * rows_out * 2)
        block = ((core * rows_out + y) * across + x) * levels + level
        places.append(block * total + start + row)
        start += rows
    return jnp.concatenate(places) if len(places) > 1 else places[0]


def permutation(row_counts, lines):
    index = relative_index(row_counts, lines)
    return (index[:, None] == jnp.arange(index.shape[0])[None, :]).astype(jnp.bfloat16)


def to_relative(low, order):
    return matmul(low, order).astype(jnp.bfloat16)


def from_relative(wide, order):
    high = lax.reduce_precision(wide, 8, 7)
    rest = wide - high
    return back_product(high.astype(jnp.bfloat16), order) + back_product(
        rest.astype(jnp.bfloat16), order
    )


def product_rel(low_rel, weights):
    own, other = weights
    half = own.shape[0]
    return matmul(low_rel[:, :half], own) + matmul(low_rel[:, half:], other)


def back_rel(grad, weights):
    own, other = weights
    return jnp.concatenate([back_product(grad, own), back_product(grad, other)], axis=1)


def owed(left, grad, lines, last_by_level):
    levels = lines["z"][2]
    half = left.shape[1] // 2
    block = half // len(offsets(lines))
    theirs = rows_product(left[:, half:], grad).astype(jnp.bfloat16)
    received = yield shift_along(theirs, lines["core"], 1)
    pieces = []
    for k, (y, x) in enumerate(offsets(lines)):
        rows = slice(k * block, (k + 1) * block)
        piece = rows_product(left[:, rows], grad) + received[rows].astype(jnp.float32)
        if k:
            piece = shift_piece(piece.astype(jnp.bfloat16), lines, y, x)
        pieces.append(piece)
    pieces = yield pieces
    if last_by_level:
        rows = block // levels
        parts = []
        for k in range(levels):
            start = (place_on(lines["z"]) + k) % levels * rows
            total = sum(
                lax.dynamic_slice_in_dim(piece, start, rows).astype(jnp.float32)
                for piece in pieces
            )
            if k:
                total = shift_along(total.astype(jnp.bfloat16), lines["z"], k)
            parts.append(total)
        parts = yield parts
        yield sum(part.astype(jnp.float32) for part in parts)
    else:
        total = sum(piece.astype(jnp.float32) for piece in pieces).astype(jnp.bfloat16)
        yield lax.psum_scatter(
            total,
            "dp",
            scatter_dimension=0,
            axis_index_groups=level_groups(lines["z"]),
            tiled=True,
        ).astype(jnp.float32)


def sum_everywhere(x):
    for axis in ("dp", "seq"):
        size = lax.axis_size(axis)
        step = 1
        while step < size:
            x = x + lax.ppermute(x, axis, [(i, i ^ step) for i in range(size)])
            step *= 2
    return x


def from_earlier(x, by):
    return passed_along(x, "seq", by)


def body(
    inputs,
    segments,
    cotangent,
    mixer_gate,
    mixer_input,
    mixer_step,
    mixer_output,
    query_weight,
    key_weight,
    value_weight,
    output_weight,
    gate_weight,
    up_weight,
    down_weight,
    input_gain,
    second_gain,
    mixer_gain,
    filter_taps,
    filter_bias,
    decay_log,
    step_bias,
    skip_gain,
):
    piece_index = lax.axis_index("seq")
    local_len = inputs.shape[1]
    seq_len = segments.shape[1]
    first_token = piece_index * local_len
    all_segs = segments[0]
    own_segments = lax.dynamic_slice_in_dim(all_segs, first_token, local_len)
    rim_start = jnp.maximum(first_token - (CONV - 1), 0)
    rim_segments = jnp.where(
        piece_index > 0, lax.dynamic_slice_in_dim(all_segs, rim_start, CONV - 1), -1
    )
    seg_before = rim_segments[CONV - 2]
    positions = first_token + jnp.arange(local_len)
    ext_segments = jnp.concatenate([rim_segments, own_segments])
    pieces = lax.axis_size("seq")
    lines = mesh_lines()
    inner = SSM_HEADS * SSM_HEAD
    query_width = HEADS * HEAD
    key_width = KV_HEADS * HEAD
    conv_width = mixer_input.shape[1]
    step_pad = jnp.pad(mixer_step, ((0, 0), (0, 128 - SSM_HEADS)))
    packed_input = jnp.concatenate([mixer_input, step_pad], axis=1)
    packed_gate = jnp.concatenate([mixer_gate, query_weight, key_weight, value_weight], axis=1)
    packed_branch = jnp.concatenate(
        [jnp.concatenate([mixer_output, output_weight], axis=0), down_weight], axis=1
    )
    packed_up = jnp.concatenate([gate_weight, up_weight], axis=1)
    both_input = gather_levels(packed_input, lines)
    both_input, packed_gate = tie(both_input, packed_gate)
    both_gate = gather_levels(packed_gate, lines)
    both_gate, packed_branch = tie(both_gate, packed_branch)
    both_branch = gather_levels(packed_branch, lines)
    both_branch, packed_up = tie(both_branch, packed_up)
    both_up = gather_levels(packed_up, lines)
    (w_input,) = spread(both_input, (packed_input.shape[1],), lines)
    (w_mix,) = spread(both_gate, (packed_gate.shape[1],), lines)
    w_branch, w_down = spread(both_branch, (output_weight.shape[1],) * 2, lines)
    (w_up,) = spread(both_up, (packed_up.shape[1],), lines)
    order_tokens = permutation((mixer_gate.shape[0],), lines)
    order_branch = permutation((mixer_output.shape[0], output_weight.shape[0]), lines)
    order_hidden = permutation((down_weight.shape[0],), lines)
    tokens = inputs[0].astype(jnp.float32)
    normed, norm_back = jax.vjp(rms_scale, tokens, input_gain)
    normed_low = normed.astype(jnp.bfloat16)
    normed_rel = to_relative(normed_low, order_tokens)
    input_out = product_rel(normed_rel, w_input)
    mixed_raw = input_out[:, :conv_width].astype(jnp.bfloat16)
    step_raw = input_out[:, conv_width : conv_width + SSM_HEADS]
    mix_out = product_rel(normed_rel, w_mix)
    gate_mix = mix_out[:, :inner]
    queries = mix_out[:, inner : inner + query_width]
    keys_raw = mix_out[:, inner + query_width : inner + query_width + key_width]
    values_low = mix_out[:, inner + query_width + key_width :].astype(jnp.bfloat16)
    rim_rows = passed_along(mixed_raw[local_len - CONV + 1 :], "seq", 1)
    extended = jnp.concatenate([rim_rows, mixed_raw], axis=0).astype(jnp.float32)

    def filter_fn(ext_rows, taps, bias):
        return conv_apply(ext_rows, ext_segments, taps, bias)

    filtered, filter_back = jax.vjp(filter_fn, extended, filter_taps, filter_bias)
    filtered_low = filtered.astype(jnp.bfloat16)
    stride_in = step_raw + step_bias
    stride = jax.nn.softplus(stride_in)
    rate = -jnp.exp(decay_log)
    running = running_sum(stride * rate)
    run_rows = running.T
    stride_rows = stride.T
    final_log = running[-1]
    keep_end = (own_segments == own_segments[-1]).astype(jnp.float32)[:, None]
    end_decay = jnp.exp(final_log[None, :] - running) * keep_end
    end_weights = end_decay * stride
    carry_decay = jnp.exp(final_log) * (own_segments[-1] == seg_before).astype(jnp.float32)
    entering = (own_segments == seg_before).astype(jnp.float32)[:, None] * jnp.exp(running)
    seg_col = own_segments[:, None]
    seg_row = own_segments[None, :]
    local_out, carry_state = ssd_local(
        filtered_low, running, run_rows, stride_rows, end_weights, skip_gain, seg_col, seg_row
    )
    packed_state = packed_message(carry_state, carry_decay)
    earlier_states = [from_earlier(packed_state, d) for d in range(1, pieces)]
    ssm_out, start_rows = ssd_entering(local_out, filtered_low, entering, earlier_states)
    gated_out, gated_back = jax.vjp(gated_norm, ssm_out, gate_mix, mixer_gain)
    gated_low = gated_out.astype(jnp.bfloat16)
    cosine, sine = rotation_tables(positions)
    key_rot = turn_pair(keys_raw, cosine, sine).astype(jnp.bfloat16)
    own_keys = jnp.concatenate([key_rot, values_low], axis=1)
    all_keys = jnp.concatenate(
        [own_keys] + [from_earlier(own_keys, d) for d in range(1, pieces)], axis=0
    )
    key_positions = jnp.concatenate([positions - d * local_len for d in range(pieces)])
    key_segments = jnp.concatenate(
        [
            lax.dynamic_slice_in_dim(all_segs, jnp.maximum(first_token - d * local_len, 0), local_len)
            for d in range(pieces)
        ]
    )
    places = (
        cosine,
        sine,
        positions[:, None],
        key_positions[None, :],
        seg_col,
        key_segments[None, :],
    )
    attended_low, lse = attention(queries, all_keys, places)
    branch_rel = to_relative(jnp.concatenate([gated_low, attended_low], axis=1), order_branch)
    middle = tokens + product_rel(branch_rel, w_branch)
    second, second_back = jax.vjp(rms_scale, middle, second_gain)
    second_low = second.astype(jnp.bfloat16)
    second_rel = to_relative(second_low, order_tokens)
    hidden = product_rel(second_rel, w_up)
    gate_val = hidden[:, : gate_weight.shape[1]]
    up_val = hidden[:, gate_weight.shape[1] :]
    activated, act_back = jax.vjp(swiglu, gate_val, up_val)
    activated_low = activated.astype(jnp.bfloat16)
    activated_rel = to_relative(activated_low, order_hidden)
    result = (middle + product_rel(activated_rel, w_down)).astype(jnp.bfloat16)
    upstream = cotangent[0].astype(jnp.float32)
    upstream_low = upstream.astype(jnp.bfloat16)
    sum_down = owed(activated_rel, upstream_low, lines, False)
    down_wait = next(sum_down)
    grad_act = from_relative(back_rel(upstream_low, w_down), order_hidden)
    grad_gate_val, grad_up_val = act_back(grad_act)
    up_low = jnp.concatenate([grad_gate_val, grad_up_val], axis=1).astype(jnp.bfloat16)
    up_low, down_wait = tie(up_low, down_wait)
    down_wait = sum_down.send(down_wait)
    sum_up = owed(second_rel, up_low, lines, False)
    up_wait = next(sum_up)
    grad_second = from_relative(back_rel(up_low, w_up), order_tokens)
    grad_middle, grad_second_gain = second_back(grad_second)
    grad_middle = grad_middle + upstream
    grad_middle, up_wait = tie(grad_middle, up_wait)
    up_wait = sum_up.send(up_wait)
    branch_low = grad_middle.astype(jnp.bfloat16)
    sum_branch = owed(branch_rel, branch_low, lines, False)
    branch_wait = next(sum_branch)
    grad_branch = from_relative(back_rel(branch_low, w_branch), order_branch)
    grad_gated = grad_branch[:, :inner]
    grad_attn = grad_branch[:, inner:]
    grad_ssm, grad_zgate, grad_mixer_gain = gated_back(grad_gated)
    zgate_low = grad_zgate.astype(jnp.bfloat16)
    grad_ssm, down_wait = tie(grad_ssm, down_wait)
    grad_down = sum_down.send(down_wait)
    value_grad, grad_incoming, row_sum, col_sum, write_grad, read_grad = ssd_back(
        grad_ssm, filtered_low, running, run_rows, stride_rows, entering, skip_gain, start_rows,
        seg_col, seg_row,
    )
    packed_grad = packed_message(grad_incoming, carry_decay)
    later_grads = [from_earlier(packed_grad, -d) for d in range(1, pieces)]
    grad_attn, branch_wait, value_grad = tie(grad_attn, branch_wait, value_grad)
    branch_wait = sum_branch.send(branch_wait)
    query_low, key_part, value_part = attention_back(queries, grad_attn, lse, all_keys, places)
    keys_part = jnp.concatenate([key_part, value_part], axis=1)
    keys_total = keys_part[:local_len]
    for d in range(1, pieces):
        sent = keys_part[d * local_len : (d + 1) * local_len].astype(jnp.bfloat16)
        keys_total = keys_total + from_earlier(sent, -d).astype(jnp.float32)
    key_total = keys_total[:, :key_width]
    value_total = keys_total[:, key_width:]
    key_low = turn_pair(key_total, cosine, -sine).astype(jnp.bfloat16)
    value_low = value_total.astype(jnp.bfloat16)
    mix_low = jnp.concatenate([zgate_low, query_low, key_low, value_low], axis=1)
    sum_mix = owed(normed_rel, mix_low, lines, False)
    mix_wait = next(sum_mix)
    grad_skip = jnp.sum(
        jnp.sum(grad_ssm * filtered_low[:, :inner].astype(jnp.float32), axis=0).reshape(
            SSM_HEADS, SSM_HEAD
        ),
        axis=1,
    )
    value_grad, end_grad, write_grad, decay_grad = ssd_state_back(
        filtered_low, end_weights, value_grad, write_grad, start_rows, later_grads
    )
    grad_decay_total = decay_grad[0]
    col_part = col_sum.T
    ended = end_grad * end_weights
    grad_running = row_sum - stride * col_part - ended
    grad_final = jnp.sum(ended, axis=0) + grad_decay_total * carry_decay
    last_row = (jnp.arange(local_len) == local_len - 1).astype(jnp.float32)[:, None]
    grad_logs = later_sum(grad_running + last_row * grad_final[None, :])
    grad_stride = col_part + end_grad * end_decay + grad_logs * rate
    grad_step = grad_stride * jax.nn.sigmoid(stride_in)
    grad_decay_log = rate * jnp.sum(grad_logs * stride, axis=0)
    grad_step_bias = jnp.sum(grad_step, axis=0)
    xc_grad = jnp.concatenate([value_grad, write_grad, read_grad], axis=1)
    xc_grad, up_wait, mix_wait = tie(xc_grad, up_wait, mix_wait)
    grad_ups = sum_up.send(up_wait)
    mix_wait = sum_mix.send(mix_wait)
    grad_ext, grad_taps, grad_fbias = filter_back(xc_grad)
    returned = passed_along(grad_ext[: CONV - 1], "seq", -1)
    grad_mixed = grad_ext[CONV - 1 :] + jnp.pad(returned, ((local_len - CONV + 1, 0), (0, 0)))
    step_pad_low = jnp.pad(grad_step.astype(jnp.bfloat16), ((0, 0), (0, 128 - SSM_HEADS)))
    input_low = jnp.concatenate([grad_mixed.astype(jnp.bfloat16), step_pad_low], axis=1)
    input_low, branch_wait = tie(input_low, branch_wait)
    grad_branch_rows = sum_branch.send(branch_wait)
    sum_input = owed(normed_rel, input_low, lines, True)
    input_wait = next(sum_input)
    input_wait = sum_input.send(input_wait)
    mix_wait, input_wait = tie(mix_wait, input_wait)
    grad_mix = sum_mix.send(mix_wait)
    grad_normed = from_relative(
        back_rel(input_low, w_input) + back_rel(mix_low, w_mix), order_tokens
    )
    input_wait = sum_input.send(input_wait)
    grad_inputs = sum_input.send(input_wait)
    mixer_rows = mixer_output.shape[0]
    mixer_grads = (
        grad_mix[:, :inner],
        grad_inputs[:, :conv_width],
        grad_inputs[:, conv_width : conv_width + SSM_HEADS],
        grad_branch_rows[:mixer_rows],
        grad_mix[:, inner : inner + query_width],
        grad_mix[:, inner + query_width : inner + query_width + key_width],
        grad_mix[:, inner + query_width + key_width :],
        grad_branch_rows[mixer_rows:],
    )
    ffn_grads = (grad_ups[:, : gate_weight.shape[1]], grad_ups[:, gate_weight.shape[1] :], grad_down)
    grad_tokens, grad_input_gain = norm_back(grad_normed)
    grad_tokens = grad_tokens + grad_middle
    small = (
        grad_input_gain,
        grad_second_gain,
        grad_mixer_gain,
        grad_taps,
        grad_fbias,
        grad_decay_log,
        grad_step_bias,
        grad_skip,
    )
    sizes = [part.size for part in small]
    length = sum(sizes)
    flat = jnp.pad(
        jnp.concatenate([part.reshape(-1) for part in small]), (0, -length % 1024)
    ).reshape(-1, 128)
    flat = sum_everywhere(flat).reshape(-1)
    small_sums = []
    start = 0
    for part in small:
        small_sums.append(flat[start : start + part.size].reshape(part.shape))
        start += part.size
    return (
        result[None],
        grad_tokens[None],
        mixer_grads[0],
        mixer_grads[1],
        mixer_grads[2],
        mixer_grads[3],
        mixer_grads[4],
        mixer_grads[5],
        mixer_grads[6],
        mixer_grads[7],
        ffn_grads[0],
        ffn_grads[1],
        ffn_grads[2],
        small_sums[0],
        small_sums[1],
        small_sums[2],
        small_sums[3],
        small_sums[4],
        small_sums[5],
        small_sums[6],
        small_sums[7],
    )


def solution(mesh):
    placed = (
        P("dp", "seq", None),
        P("dp", None),
        P("dp", "seq", None),
        P(("dp", "seq"), None),
        P(("dp", "seq"), None),
        P(("dp", "seq"), None),
        P(("dp", "seq"), None),
        P(("dp", "seq"), None),
        P(("dp", "seq"), None),
        P(("dp", "seq"), None),
        P(("dp", "seq"), None),
        P(("dp", "seq"), None),
        P(("dp", "seq"), None),
        P(("dp", "seq"), None),
        P(),
        P(),
        P(),
        P(),
        P(),
        P(),
        P(),
        P(),
    )
    return jax.shard_map(
        body,
        mesh=mesh,
        in_specs=placed,
        out_specs=(
            P("dp", "seq", None),
            P("dp", "seq", None),
            P(("dp", "seq"), None),
            P(("dp", "seq"), None),
            P(("dp", "seq"), None),
            P(("dp", "seq"), None),
            P(("dp", "seq"), None),
            P(("dp", "seq"), None),
            P(("dp", "seq"), None),
            P(("dp", "seq"), None),
            P(("dp", "seq"), None),
            P(("dp", "seq"), None),
            P(("dp", "seq"), None),
            P(),
            P(),
            P(),
            P(),
            P(),
            P(),
            P(),
            P(),
        ),
        check_vma=False,
    )
```

```python
import functools

import jax
import jax.numpy as jnp
from jax import lax
from jax.experimental import pallas as pl
from jax.experimental.pallas import tpu as pltpu
from jax.sharding import PartitionSpec as P

HEADS = 8
KV_HEADS = 2
HEAD = 64
SSM_HEADS = 24
SSM_HEAD = 64
STATE = 128
CONV = 4


eps = 1e-05
rope_theta = 100000000000.0
score_scale = 0.125


def passed_along(x, axis, by):
    length = lax.axis_size(axis)
    pairs = [(i, i + by) for i in range(length) if 0 <= i + by < length]
    return lax.ppermute(x, axis, pairs)


def matmul(left, right):
    return jnp.dot(left, right, preferred_element_type=jnp.float32)


def rows_product(left, right):
    return lax.dot_general(
        left, right, (((0,), (0,)), ((), ())), preferred_element_type=jnp.float32
    )


def back_product(left, right):
    return lax.dot_general(
        left, right, (((1,), (1,)), ((), ())), preferred_element_type=jnp.float32
    )


def rms_scale(tensor, scale_gain):
    return tensor * lax.rsqrt(jnp.mean(tensor * tensor, axis=-1, keepdims=True) + eps) * scale_gain


def rotation_tables(positions):
    half_width = HEAD // 2
    frequency = rope_theta ** (-jnp.arange(half_width, dtype=jnp.float32) / half_width)
    angle = positions.astype(jnp.float32)[:, None] * frequency[None, :]
    cosine = jnp.cos(angle)
    sine = jnp.sin(angle)
    return (
        jnp.concatenate([cosine] * 4, axis=1),
        jnp.concatenate([-sine, sine, -sine, sine], axis=1),
    )


def conv_apply(extended, ext_segments, filter_taps, filter_bias):
    length = extended.shape[0] - CONV + 1
    own_segment = ext_segments[CONV - 1 :]
    summed = jnp.zeros((length, extended.shape[1]), jnp.float32) + filter_bias[None, :]
    for offset in range(CONV):
        match_mask = (ext_segments[offset : offset + length] == own_segment).astype(jnp.float32)[
            :, None
        ]
        summed = (
            summed + filter_taps[offset][None, :] * extended[offset : offset + length] * match_mask
        )
    return jax.nn.silu(summed)


def running_sum(x):
    order = jnp.arange(x.shape[0])
    earlier = (order[:, None] >= order[None, :]).astype(jnp.float32)
    return jnp.dot(earlier, x, precision=lax.Precision.HIGHEST)


def later_sum(x):
    order = jnp.arange(x.shape[0])
    later = (order[:, None] <= order[None, :]).astype(jnp.float32)
    return jnp.dot(later, x, precision=lax.Precision.HIGHEST)


PAIR = 128
DECAY_ROWS = 32


def dot_nn(left, right):
    return jnp.dot(left, right, preferred_element_type=jnp.float32)


def dot_nt(left, right):
    return lax.dot_general(
        left, right, (((1,), (1,)), ((), ())), preferred_element_type=jnp.float32
    )


def dot_tn(left, right):
    return lax.dot_general(
        left, right, (((0,), (0,)), ((), ())), preferred_element_type=jnp.float32
    )


def low(x):
    return x.astype(jnp.bfloat16)


def lane_index(shape):
    return lax.broadcasted_iota(jnp.int32, shape, 1)


def column_of(table, index):
    return jnp.sum(jnp.where(lane_index(table.shape) == index, table, 0.0), axis=1, keepdims=True)


def set_column(ref, index, column):
    table = ref[...]
    ref[...] = jnp.where(lane_index(table.shape) == index, column, table)


def by_head(first, second, shape):
    return jnp.where(lane_index(shape) < HEAD, first, second)


def whole_spec(shape):
    return pl.BlockSpec(shape, lambda i: (0,) * len(shape))


def pair_spec(rows):
    return pl.BlockSpec((rows, PAIR), lambda i: (0, i))


def state_spec():
    return pl.BlockSpec((PAIR, STATE), lambda i: (i, 0))


def call(kernel, grid, in_specs, out_specs, out_shape, scratch=(), flops=0):
    return pl.pallas_call(
        kernel,
        grid=(grid,),
        in_specs=in_specs,
        out_specs=out_specs,
        out_shape=out_shape,
        scratch_shapes=list(scratch),
        compiler_params=pltpu.CompilerParams(
            dimension_semantics=("arbitrary",), vmem_limit_bytes=24 * 1024 * 1024
        ),
        cost_estimate=pl.CostEstimate(flops=flops, bytes_accessed=4000000, transcendentals=0),
    )


def float_out(*shape):
    return jax.ShapeDtypeStruct(shape, jnp.float32)


def masked_products(read_ref, write_ref, seg_col, seg_row):
    products = dot_nt(read_ref[...], write_ref[...])
    row = lax.broadcasted_iota(jnp.int32, products.shape, 0)
    allowed = (row >= lane_index(products.shape)) & (seg_col[...] == seg_row[...])
    return jnp.where(allowed, products, 0.0)


def ssd_local_kernel(
    value_ref, write_ref, read_ref, run_ref, run_row, stride_row, end_ref, skip_ref, seg_col,
    seg_row, out_ref, state_ref, products,
):
    step = pl.program_id(0)

    @pl.when(step == 0)
    def _():
        products[...] = masked_products(read_ref, write_ref, seg_col, seg_row)

    value = value_ref[...]
    wide = value.astype(jnp.float32)
    outs = []
    for half in range(2):
        head = 2 * step + half
        gap = column_of(run_ref[...], head) - run_row[pl.ds(head, 1), :]
        mixing = jnp.exp(jnp.minimum(gap, 0.0)) * products[...] * stride_row[pl.ds(head, 1), :]
        outs.append(dot_nn(low(mixing), value))
    skip = by_head(
        column_of(skip_ref[...], 2 * step), column_of(skip_ref[...], 2 * step + 1), (1, PAIR)
    )
    out_ref[...] = by_head(outs[0], outs[1], wide.shape) + skip * wide
    weight = by_head(
        column_of(end_ref[...], 2 * step), column_of(end_ref[...], 2 * step + 1), wide.shape
    )
    state_ref[...] = dot_tn(low(weight * wide), write_ref[...])


def ssd_local(filtered, running, run_rows, stride_rows, end_weights, skip_gain, seg_col, seg_row):
    length = filtered.shape[0]
    pairs = SSM_HEADS // 2
    inner = SSM_HEADS * SSM_HEAD
    return call(
        ssd_local_kernel,
        pairs,
        [
            pair_spec(length),
            pl.BlockSpec((length, STATE), lambda i: (0, pairs)),
            pl.BlockSpec((length, STATE), lambda i: (0, pairs + 1)),
            whole_spec((length, SSM_HEADS)),
            whole_spec((SSM_HEADS, length)),
            whole_spec((SSM_HEADS, length)),
            whole_spec((length, SSM_HEADS)),
            whole_spec((1, SSM_HEADS)),
            whole_spec((length, 1)),
            whole_spec((1, length)),
        ],
        [pair_spec(length), state_spec()],
        [float_out(length, inner), float_out(inner, STATE)],
        [pltpu.VMEM((length, length), jnp.float32)],
        2 * SSM_HEADS * length * length * PAIR,
    )(
        filtered, filtered, filtered, running, run_rows, stride_rows, end_weights,
        skip_gain[None, :], seg_col, seg_row,
    )


def chained(message_refs, step):
    first = (lax.broadcasted_iota(jnp.int32, (PAIR, STATE), 0) // SSM_HEAD) == 0
    state = jnp.zeros((PAIR, STATE), jnp.float32)
    for block_ref, decay_ref in reversed(message_refs):
        decays = decay_ref[...].astype(jnp.float32)
        row = lax.broadcasted_iota(jnp.int32, decays.shape, 0)
        one = jnp.sum(jnp.where(row == 2 * step, decays, 0.0), axis=0, keepdims=True)
        two = jnp.sum(jnp.where(row == 2 * step + 1, decays, 0.0), axis=0, keepdims=True)
        state = jnp.where(first, one, two) * state + block_ref[...].astype(jnp.float32)
    return state


def message_specs(count):
    blocks = SSM_HEADS * SSM_HEAD // DECAY_ROWS
    return [
        spec
        for _ in range(count)
        for spec in (state_spec(), pl.BlockSpec((DECAY_ROWS, STATE), lambda i: (blocks, 0)))
    ]


def packed_message(states, decays):
    rows = jnp.broadcast_to(jnp.pad(decays, (0, DECAY_ROWS - SSM_HEADS))[:, None], (DECAY_ROWS, STATE))
    return jnp.concatenate([low(states), low(rows)])


def ssd_entering_kernel(local_ref, read_ref, enter_ref, *refs):
    message_refs, (out_ref, state_ref) = (refs[:-2], refs[-2:])
    step = pl.program_id(0)
    shape = local_ref.shape
    state_ref[...] = chained(list(zip(message_refs[::2], message_refs[1::2])), step)
    enter = by_head(
        column_of(enter_ref[...], 2 * step), column_of(enter_ref[...], 2 * step + 1), shape
    )
    out_ref[...] = local_ref[...] + enter * dot_nt(read_ref[...], low(state_ref[...]))


def ssd_entering(local, filtered, entering, messages):
    length = filtered.shape[0]
    pairs = SSM_HEADS // 2
    inner = SSM_HEADS * SSM_HEAD
    return call(
        ssd_entering_kernel,
        pairs,
        [
            pair_spec(length),
            pl.BlockSpec((length, STATE), lambda i: (0, pairs + 1)),
            whole_spec((length, SSM_HEADS)),
        ]
        + message_specs(len(messages)),
        [pair_spec(length), state_spec()],
        [float_out(*local.shape), float_out(inner, STATE)],
        (),
        2 * SSM_HEADS * length * STATE * SSM_HEAD,
    )(local, filtered, entering, *[m for message in messages for m in (message, message)])


def ssd_back_kernel(
    grad_ref, value_ref, write_ref, read_ref, run_ref, run_row, stride_row, enter_ref, skip_ref,
    state_ref, seg_col, seg_row, value_grad, state_grad, row_sum, col_sum, write_grad, read_grad,
    products, total,
):
    step = pl.program_id(0)

    @pl.when(step == 0)
    def _():
        products[...] = masked_products(read_ref, write_ref, seg_col, seg_row)
        total[...] = jnp.zeros_like(total)
        row_sum[...] = jnp.zeros_like(row_sum)
        read_grad[...] = jnp.zeros_like(read_grad)

    value = value_ref[...]
    grad = grad_ref[...]
    shape = grad.shape
    skip = by_head(
        column_of(skip_ref[...], 2 * step), column_of(skip_ref[...], 2 * step + 1), (1, PAIR)
    )
    enter = by_head(
        column_of(enter_ref[...], 2 * step), column_of(enter_ref[...], 2 * step + 1), shape
    )
    state = low(state_ref[...])
    read = read_ref[...]
    entered = enter * grad
    from_state = entered * dot_nt(read, state)
    entered = low(entered)
    state_grad[...] = dot_tn(entered, read)
    read_grad[...] += dot_nn(entered, state)
    into_values = skip * grad
    for half in range(2):
        head = 2 * step + half
        inside = (lane_index(shape) // HEAD) == half
        part = low(jnp.where(inside, grad, 0.0))
        gap = column_of(run_ref[...], head) - run_row[pl.ds(head, 1), :]
        decay = jnp.exp(jnp.minimum(gap, 0.0))
        strides = stride_row[pl.ds(head, 1), :]
        weighted = dot_nt(part, value) * decay
        total[...] += weighted * strides
        scaled = weighted * products[...]
        col_sum[pl.ds(head, 1), :] = jnp.sum(scaled, axis=0, keepdims=True)
        rows = jnp.sum(scaled * strides, axis=1, keepdims=True) + jnp.sum(
            jnp.where(inside, from_state, 0.0), axis=1, keepdims=True
        )
        set_column(row_sum, head, rows)
        mixing = decay * products[...] * strides
        into_values = into_values + dot_tn(low(mixing), part)
    value_grad[...] = into_values

    @pl.when(step == pl.num_programs(0) - 1)
    def _():
        sums = total[...]
        row = lax.broadcasted_iota(jnp.int32, sums.shape, 0)
        allowed = (row >= lane_index(sums.shape)) & (seg_col[...] == seg_row[...])
        sums = low(jnp.where(allowed, sums, 0.0))
        write_grad[...] = dot_tn(sums, read)
        read_grad[...] += dot_nn(sums, write_ref[...])


def ssd_back(
    grad, filtered, running, run_rows, stride_rows, entering, skip_gain, state, seg_col, seg_row
):
    length = filtered.shape[0]
    pairs = SSM_HEADS // 2
    inner = SSM_HEADS * SSM_HEAD
    return call(
        ssd_back_kernel,
        pairs,
        [
            pair_spec(length),
            pair_spec(length),
            pl.BlockSpec((length, STATE), lambda i: (0, pairs)),
            pl.BlockSpec((length, STATE), lambda i: (0, pairs + 1)),
            whole_spec((length, SSM_HEADS)),
            whole_spec((SSM_HEADS, length)),
            whole_spec((SSM_HEADS, length)),
            whole_spec((length, SSM_HEADS)),
            whole_spec((1, SSM_HEADS)),
            state_spec(),
            whole_spec((length, 1)),
            whole_spec((1, length)),
        ],
        [
            pair_spec(length),
            state_spec(),
            whole_spec((length, SSM_HEADS)),
            whole_spec((SSM_HEADS, length)),
            whole_spec((length, STATE)),
            whole_spec((length, STATE)),
        ],
        [
            float_out(length, inner),
            float_out(inner, STATE),
            float_out(length, SSM_HEADS),
            float_out(SSM_HEADS, length),
            float_out(length, STATE),
            float_out(length, STATE),
        ],
        [pltpu.VMEM((length, length), jnp.float32), pltpu.VMEM((length, length), jnp.float32)],
        4 * SSM_HEADS * length * length * PAIR,
    )(
        grad, filtered, filtered, filtered, running, run_rows, stride_rows, entering,
        skip_gain[None, :], state, seg_col, seg_row,
    )


def ssd_state_back_kernel(
    value_ref, write_ref, end_ref, before_ref, write_before, start_ref, *refs
):
    message_refs, (value_grad, end_grad, write_grad, decay_grad) = (refs[:-4], refs[-4:])
    step = pl.program_id(0)

    @pl.when(step == 0)
    def _():
        end_grad[...] = jnp.zeros_like(end_grad)
        write_grad[...] = write_before[...]
        decay_grad[...] = jnp.zeros_like(decay_grad)

    wide = value_ref[...].astype(jnp.float32)
    shape = wide.shape
    weight = by_head(
        column_of(end_ref[...], 2 * step), column_of(end_ref[...], 2 * step + 1), shape
    )
    carried = chained(list(zip(message_refs[::2], message_refs[1::2])), step)
    products = jnp.sum(carried * start_ref[...], axis=1, keepdims=True)
    first = lax.broadcasted_iota(jnp.int32, products.shape, 0) // SSM_HEAD == 0
    head = lane_index(decay_grad.shape)
    for half in range(2):
        total = jnp.sum(jnp.where(first == (half == 0), products, 0.0), axis=0, keepdims=True)
        decay_grad[...] = jnp.where(head == 2 * step + half, total, decay_grad[...])
    carried = low(carried)
    reached = dot_nt(write_ref[...], carried)
    value_grad[...] = before_ref[...] + weight * reached
    write_grad[...] += dot_nn(low(weight * wide), carried)
    product = wide * reached
    for half in range(2):
        inside = (lane_index(shape) // HEAD) == half
        set_column(
            end_grad,
            2 * step + half,
            jnp.sum(jnp.where(inside, product, 0.0), axis=1, keepdims=True),
        )


def ssd_state_back(filtered, end_weights, value_before, write_before, start, messages):
    length = filtered.shape[0]
    pairs = SSM_HEADS // 2
    return call(
        ssd_state_back_kernel,
        pairs,
        [
            pair_spec(length),
            pl.BlockSpec((length, STATE), lambda i: (0, pairs)),
            whole_spec((length, SSM_HEADS)),
            pair_spec(length),
            whole_spec((length, STATE)),
            state_spec(),
        ]
        + message_specs(len(messages)),
        [
            pair_spec(length),
            whole_spec((length, SSM_HEADS)),
            whole_spec((length, STATE)),
            whole_spec((1, SSM_HEADS)),
        ],
        [
            float_out(*value_before.shape),
            float_out(length, SSM_HEADS),
            float_out(length, STATE),
            float_out(1, SSM_HEADS),
        ],
        (),
        4 * SSM_HEADS * length * STATE * SSM_HEAD,
    )(
        filtered, filtered, end_weights, value_before, write_before, start,
        *[m for message in messages for m in (message, message)],
    )


def turned(x, cosine, sine):
    quarter = HEAD // 2
    after = pltpu.roll(x, x.shape[1] - quarter, 1)
    earlier = pltpu.roll(x, quarter, 1)
    other = jnp.where(lane_index(x.shape) % HEAD < quarter, after, earlier)
    return x * cosine + other * sine


def group_rows(both, group):
    wide = both.astype(jnp.float32)
    kept = jnp.where(lane_index(wide.shape) // HEAD == group, wide, 0.0)
    return low(kept + pltpu.roll(kept, HEAD, 1))


def attention_mask(bias, pos_col, pos_row, seg_col, seg_row):
    allowed = (
        (pos_row[...] <= pos_col[...]) & (pos_row[...] >= 0) & (seg_row[...] == seg_col[...])
    )
    bias[...] = jnp.where(allowed, 0.0, -1e30)


def attention_kernel(
    query_ref, keys_ref, values_ref, cos_ref, sin_ref, pos_col, pos_row, seg_col, seg_row, out_ref,
    lse_ref, bias,
):
    step = pl.program_id(0)

    @pl.when(step == 0)
    def _():
        attention_mask(bias, pos_col, pos_row, seg_col, seg_row)
        lse_ref[...] = jnp.zeros_like(lse_ref)

    group = step * 2 // (HEADS // KV_HEADS)
    keys = group_rows(keys_ref[...], group)
    values = group_rows(values_ref[...], group)
    query = low(turned(query_ref[...], cos_ref[...], sin_ref[...])).astype(jnp.float32)
    outs = []
    for half in range(2):
        inside = (lane_index(query.shape) // HEAD) == half
        part = low(jnp.where(inside, query, 0.0))
        scores = dot_nt(part, keys) * score_scale + bias[...]
        top = jnp.max(scores, axis=1, keepdims=True)
        lse = top + jnp.log(jnp.sum(jnp.exp(scores - top), axis=1, keepdims=True))
        outs.append(dot_nn(low(jnp.exp(scores - lse)), values))
        set_column(lse_ref, 2 * step + half, lse)
    out_ref[...] = low(by_head(outs[0], outs[1], query.shape))


def attention_specs(length, keys):
    return [
        whole_spec((length, PAIR)),
        whole_spec((length, PAIR)),
        whole_spec((length, 1)),
        whole_spec((1, keys)),
        whole_spec((length, 1)),
        whole_spec((1, keys)),
    ]


def attention(queries, all_keys, places):
    length = queries.shape[0]
    keys = all_keys.shape[0]
    return call(
        attention_kernel,
        HEADS // 2,
        [
            pair_spec(length),
            pl.BlockSpec((keys, PAIR), lambda i: (0, 0)),
            pl.BlockSpec((keys, PAIR), lambda i: (0, 1)),
        ]
        + attention_specs(length, keys),
        [pair_spec(length), whole_spec((length, HEADS))],
        [jax.ShapeDtypeStruct(queries.shape, jnp.bfloat16), float_out(length, HEADS)],
        [pltpu.VMEM((length, keys), jnp.float32)],
        4 * HEADS * length * keys * PAIR,
    )(queries, all_keys, all_keys, *places)


def attention_back_kernel(
    query_ref, grad_ref, lse_ref, keys_ref, values_ref, cos_ref, sin_ref, pos_col, pos_row,
    seg_col, seg_row, query_grad, key_grad, value_grad, bias,
):
    step = pl.program_id(0)

    @pl.when(step == 0)
    def _():
        attention_mask(bias, pos_col, pos_row, seg_col, seg_row)
        key_grad[...] = jnp.zeros_like(key_grad)
        value_grad[...] = jnp.zeros_like(value_grad)

    group = step * 2 // (HEADS // KV_HEADS)
    keys = group_rows(keys_ref[...], group)
    values = group_rows(values_ref[...], group)
    query = low(turned(query_ref[...], cos_ref[...], sin_ref[...])).astype(jnp.float32)
    grad = low(grad_ref[...]).astype(jnp.float32)
    into_query = []
    into_keys = jnp.zeros(key_grad.shape, jnp.float32)
    into_values = jnp.zeros(key_grad.shape, jnp.float32)
    for half in range(2):
        inside = (lane_index(query.shape) // HEAD) == half
        part = low(jnp.where(inside, query, 0.0))
        grad_part = low(jnp.where(inside, grad, 0.0))
        scores = dot_nt(part, keys) * score_scale + bias[...]
        probs = jnp.exp(scores - column_of(lse_ref[...], 2 * step + half))
        grad_probs = dot_nt(grad_part, values)
        delta = jnp.sum(probs * grad_probs, axis=1, keepdims=True)
        grad_scores = low(probs * (grad_probs - delta))
        into_query.append(dot_nn(grad_scores, keys))
        into_keys = into_keys + dot_tn(grad_scores, part)
        into_values = into_values + dot_tn(low(probs), grad_part)
    wide = by_head(into_query[0], into_query[1], query.shape) * score_scale
    query_grad[...] = low(turned(wide, cos_ref[...], -sin_ref[...]))
    mine = lane_index(into_keys.shape) // HEAD == group
    into_keys = into_keys + pltpu.roll(into_keys, HEAD, 1)
    into_values = into_values + pltpu.roll(into_values, HEAD, 1)
    key_grad[...] += jnp.where(mine, into_keys * score_scale, 0.0)
    value_grad[...] += jnp.where(mine, into_values, 0.0)


def attention_back(queries, grads, lse, all_keys, places):
    length = queries.shape[0]
    keys = all_keys.shape[0]
    return call(
        attention_back_kernel,
        HEADS // 2,
        [
            pair_spec(length),
            pair_spec(length),
            whole_spec((length, HEADS)),
            pl.BlockSpec((keys, PAIR), lambda i: (0, 0)),
            pl.BlockSpec((keys, PAIR), lambda i: (0, 1)),
        ]
        + attention_specs(length, keys),
        [pair_spec(length), whole_spec((keys, PAIR)), whole_spec((keys, PAIR))],
        [
            jax.ShapeDtypeStruct(queries.shape, jnp.bfloat16),
            float_out(keys, PAIR),
            float_out(keys, PAIR),
        ],
        [pltpu.VMEM((length, keys), jnp.float32)],
        10 * HEADS * length * keys * PAIR,
    )(queries, grads, lse, all_keys, all_keys, *places)


def turn_pair(x, cosine, sine):
    quarter = HEAD // 2
    pieces = [x[:, k * quarter : (k + 1) * quarter] for k in range(x.shape[1] // quarter)]
    other = jnp.concatenate([pieces[k ^ 1] for k in range(len(pieces))], axis=1)
    return x * cosine + other * sine


def gated_norm(ssm_out, gate_mix, mixer_gain):
    return rms_scale(ssm_out * jax.nn.silu(gate_mix), mixer_gain)


def swiglu(gate_val, up_val):
    return jax.nn.silu(gate_val) * up_val


def shift_along(x, line, by):
    axis, stride, size = line
    pairs = []
    for index in range(lax.axis_size(axis)):
        place = (index // stride) % size
        pairs.append((index, index + ((place + by) % size - place) * stride))
    return lax.ppermute(x, axis, pairs)


def mesh_lines():
    replicas, pieces = (lax.axis_size("dp"), lax.axis_size("seq"))
    across = 1
    while across * across * 2 <= pieces:
        across *= 2
    lines = {
        "core": ("dp", 1, 2),
        "z": ("dp", 2, replicas // 2),
        "x": ("seq", 1, across),
        "y": ("seq", across, pieces // across),
    }
    return lines


def place_on(line):
    axis, stride, size = line
    return (lax.axis_index(axis) // stride) % size


def tie(*groups):
    return lax.optimization_barrier(groups)


def shift_piece(x, lines, down, right):
    rows, across = (lines["y"][2], lines["x"][2])
    pairs = []
    for index in range(rows * across):
        y, x_place = (index // across, index % across)
        pairs.append((index, (y + down) % rows * across + (x_place + right) % across))
    return lax.ppermute(x, "seq", pairs)


def offsets(lines):
    return [(y, x) for y in range(lines["y"][2]) for x in range(lines["x"][2])]


def level_groups(line):
    axis, stride, size = line
    return [[c + stride * k for k in range(size)] for c in range(stride)]


def gather_levels(packed, lines):
    return lax.all_gather(packed, "dp")


def spread(both, widths, lines):
    levels, rows, width = (lines["z"][2], both.shape[1], both.shape[2])
    mine = lax.dynamic_index_in_dim(
        both.reshape(levels, 2, rows, width), place_on(lines["core"]), 1, False
    ).reshape(levels * rows, width)
    blocks = [shift_piece(mine, lines, -y, -x) if y or x else mine for y, x in offsets(lines)]
    found = []
    start = 0
    for size in widths:
        own = jnp.concatenate([block[:, start : start + size] for block in blocks], axis=0)
        found.append((own, shift_along(own, lines["core"], 1)))
        start += size
    return found


def relative_index(row_counts, lines):
    levels, rows_out, across = (lines["z"][2], lines["y"][2], lines["x"][2])
    total = sum(row_counts)
    places = []
    start = 0
    for rows in row_counts:
        column = jnp.arange(levels * 2 * rows_out * across * rows)
        row = column % rows
        device = column // rows
        x = (device % across - place_on(lines["x"])) % across
        y = (device // across % rows_out - place_on(lines["y"])) % rows_out
        core = (device // (across * rows_out) - place_on(lines["core"])) % 2
        level = device // (across * rows_out * 2)
        block = ((core * rows_out + y) * across + x) * levels + level
        places.append(block * total + start + row)
        start += rows
    return jnp.concatenate(places) if len(places) > 1 else places[0]


def permutation(row_counts, lines):
    index = relative_index(row_counts, lines)
    return (index[:, None] == jnp.arange(index.shape[0])[None, :]).astype(jnp.bfloat16)


def to_relative(low, order):
    return matmul(low, order).astype(jnp.bfloat16)


def from_relative(wide, order):
    high = lax.reduce_precision(wide, 8, 7)
    rest = wide - high
    return back_product(high.astype(jnp.bfloat16), order) + back_product(
        rest.astype(jnp.bfloat16), order
    )


def product_rel(low_rel, weights):
    own, other = weights
    half = own.shape[0]
    return matmul(low_rel[:, :half], own) + matmul(low_rel[:, half:], other)


def back_rel(grad, weights):
    own, other = weights
    return jnp.concatenate([back_product(grad, own), back_product(grad, other)], axis=1)


def owed(left, grad, lines, last_by_level):
    levels = lines["z"][2]
    half = left.shape[1] // 2
    block = half // len(offsets(lines))
    theirs = rows_product(left[:, half:], grad).astype(jnp.bfloat16)
    received = yield shift_along(theirs, lines["core"], 1)
    pieces = []
    for k, (y, x) in enumerate(offsets(lines)):
        rows = slice(k * block, (k + 1) * block)
        piece = rows_product(left[:, rows], grad) + received[rows].astype(jnp.float32)
        if k:
            piece = shift_piece(piece.astype(jnp.bfloat16), lines, y, x)
        pieces.append(piece)
    pieces = yield pieces
    if last_by_level:
        rows = block // levels
        parts = []
        for k in range(levels):
            start = (place_on(lines["z"]) + k) % levels * rows
            total = sum(
                lax.dynamic_slice_in_dim(piece, start, rows).astype(jnp.float32)
                for piece in pieces
            )
            if k:
                total = shift_along(total.astype(jnp.bfloat16), lines["z"], k)
            parts.append(total)
        parts = yield parts
        yield sum(part.astype(jnp.float32) for part in parts)
    else:
        total = sum(piece.astype(jnp.float32) for piece in pieces).astype(jnp.bfloat16)
        yield lax.psum_scatter(
            total,
            "dp",
            scatter_dimension=0,
            axis_index_groups=level_groups(lines["z"]),
            tiled=True,
        ).astype(jnp.float32)


def sum_everywhere(x):
    for axis in ("dp", "seq"):
        size = lax.axis_size(axis)
        step = 1
        while step < size:
            x = x + lax.ppermute(x, axis, [(i, i ^ step) for i in range(size)])
            step *= 2
    return x


def from_earlier(x, by):
    return passed_along(x, "seq", by)


def body(
    inputs,
    segments,
    cotangent,
    mixer_gate,
    mixer_input,
    mixer_step,
    mixer_output,
    query_weight,
    key_weight,
    value_weight,
    output_weight,
    gate_weight,
    up_weight,
    down_weight,
    input_gain,
    second_gain,
    mixer_gain,
    filter_taps,
    filter_bias,
    decay_log,
    step_bias,
    skip_gain,
):
    piece_index = lax.axis_index("seq")
    local_len = inputs.shape[1]
    seq_len = segments.shape[1]
    first_token = piece_index * local_len
    all_segs = segments[0]
    own_segments = lax.dynamic_slice_in_dim(all_segs, first_token, local_len)
    rim_start = jnp.maximum(first_token - (CONV - 1), 0)
    rim_segments = jnp.where(
        piece_index > 0, lax.dynamic_slice_in_dim(all_segs, rim_start, CONV - 1), -1
    )
    seg_before = rim_segments[CONV - 2]
    positions = first_token + jnp.arange(local_len)
    ext_segments = jnp.concatenate([rim_segments, own_segments])
    pieces = lax.axis_size("seq")
    lines = mesh_lines()
    inner = SSM_HEADS * SSM_HEAD
    query_width = HEADS * HEAD
    key_width = KV_HEADS * HEAD
    conv_width = mixer_input.shape[1]
    step_pad = jnp.pad(mixer_step, ((0, 0), (0, 128 - SSM_HEADS)))
    packed_input = jnp.concatenate([mixer_input, step_pad], axis=1)
    packed_gate = jnp.concatenate([mixer_gate, query_weight, key_weight, value_weight], axis=1)
    packed_branch = jnp.concatenate(
        [jnp.concatenate([mixer_output, output_weight], axis=0), down_weight], axis=1
    )
    packed_up = jnp.concatenate([gate_weight, up_weight], axis=1)
    both_input = gather_levels(packed_input, lines)
    both_input, packed_gate = tie(both_input, packed_gate)
    both_gate = gather_levels(packed_gate, lines)
    both_gate, packed_branch = tie(both_gate, packed_branch)
    both_branch = gather_levels(packed_branch, lines)
    both_branch, packed_up = tie(both_branch, packed_up)
    both_up = gather_levels(packed_up, lines)
    (w_input,) = spread(both_input, (packed_input.shape[1],), lines)
    (w_mix,) = spread(both_gate, (packed_gate.shape[1],), lines)
    w_branch, w_down = spread(both_branch, (output_weight.shape[1],) * 2, lines)
    (w_up,) = spread(both_up, (packed_up.shape[1],), lines)
    order_tokens = permutation((mixer_gate.shape[0],), lines)
    order_branch = permutation((mixer_output.shape[0], output_weight.shape[0]), lines)
    order_hidden = permutation((down_weight.shape[0],), lines)
    tokens = inputs[0].astype(jnp.float32)
    normed, norm_back = jax.vjp(rms_scale, tokens, input_gain)
    normed_low = normed.astype(jnp.bfloat16)
    normed_rel = to_relative(normed_low, order_tokens)
    input_out = product_rel(normed_rel, w_input)
    mixed_raw = input_out[:, :conv_width].astype(jnp.bfloat16)
    step_raw = input_out[:, conv_width : conv_width + SSM_HEADS]
    mix_out = product_rel(normed_rel, w_mix)
    gate_mix = mix_out[:, :inner]
    queries = mix_out[:, inner : inner + query_width]
    keys_raw = mix_out[:, inner + query_width : inner + query_width + key_width]
    values_low = mix_out[:, inner + query_width + key_width :].astype(jnp.bfloat16)
    rim_rows = passed_along(mixed_raw[local_len - CONV + 1 :], "seq", 1)
    extended = jnp.concatenate([rim_rows, mixed_raw], axis=0).astype(jnp.float32)

    def filter_fn(ext_rows, taps, bias):
        return conv_apply(ext_rows, ext_segments, taps, bias)

    filtered, filter_back = jax.vjp(filter_fn, extended, filter_taps, filter_bias)
    filtered_low = filtered.astype(jnp.bfloat16)
    stride_in = step_raw + step_bias
    stride = jax.nn.softplus(stride_in)
    rate = -jnp.exp(decay_log)
    running = running_sum(stride * rate)
    run_rows = running.T
    stride_rows = stride.T
    final_log = running[-1]
    keep_end = (own_segments == own_segments[-1]).astype(jnp.float32)[:, None]
    end_decay = jnp.exp(final_log[None, :] - running) * keep_end
    end_weights = end_decay * stride
    carry_decay = jnp.exp(final_log) * (own_segments[-1] == seg_before).astype(jnp.float32)
    entering = (own_segments == seg_before).astype(jnp.float32)[:, None] * jnp.exp(running)
    seg_col = own_segments[:, None]
    seg_row = own_segments[None, :]
    local_out, carry_state = ssd_local(
        filtered_low, running, run_rows, stride_rows, end_weights, skip_gain, seg_col, seg_row
    )
    packed_state = packed_message(carry_state, carry_decay)
    earlier_states = [from_earlier(packed_state, d) for d in range(1, pieces)]
    ssm_out, start_rows = ssd_entering(local_out, filtered_low, entering, earlier_states)
    gated_out, gated_back = jax.vjp(gated_norm, ssm_out, gate_mix, mixer_gain)
    gated_low = gated_out.astype(jnp.bfloat16)
    cosine, sine = rotation_tables(positions)
    key_rot = turn_pair(keys_raw, cosine, sine).astype(jnp.bfloat16)
    own_keys = jnp.concatenate([key_rot, values_low], axis=1)
    all_keys = jnp.concatenate(
        [own_keys] + [from_earlier(own_keys, d) for d in range(1, pieces)], axis=0
    )
    key_positions = jnp.concatenate([positions - d * local_len for d in range(pieces)])
    key_segments = jnp.concatenate(
        [
            lax.dynamic_slice_in_dim(all_segs, jnp.maximum(first_token - d * local_len, 0), local_len)
            for d in range(pieces)
        ]
    )
    places = (
        cosine,
        sine,
        positions[:, None],
        key_positions[None, :],
        seg_col,
        key_segments[None, :],
    )
    attended_low, lse = attention(queries, all_keys, places)
    branch_rel = to_relative(jnp.concatenate([gated_low, attended_low], axis=1), order_branch)
    middle = tokens + product_rel(branch_rel, w_branch)
    second, second_back = jax.vjp(rms_scale, middle, second_gain)
    second_low = second.astype(jnp.bfloat16)
    second_rel = to_relative(second_low, order_tokens)
    hidden = product_rel(second_rel, w_up)
    gate_val = hidden[:, : gate_weight.shape[1]]
    up_val = hidden[:, gate_weight.shape[1] :]
    activated, act_back = jax.vjp(swiglu, gate_val, up_val)
    activated_low = activated.astype(jnp.bfloat16)
    activated_rel = to_relative(activated_low, order_hidden)
    result = (middle + product_rel(activated_rel, w_down)).astype(jnp.bfloat16)
    upstream = cotangent[0].astype(jnp.float32)
    upstream_low = upstream.astype(jnp.bfloat16)
    sum_down = owed(activated_rel, upstream_low, lines, False)
    down_wait = next(sum_down)
    grad_act = from_relative(back_rel(upstream_low, w_down), order_hidden)
    grad_gate_val, grad_up_val = act_back(grad_act)
    up_low = jnp.concatenate([grad_gate_val, grad_up_val], axis=1).astype(jnp.bfloat16)
    up_low, down_wait = tie(up_low, down_wait)
    down_wait = sum_down.send(down_wait)
    sum_up = owed(second_rel, up_low, lines, False)
    up_wait = next(sum_up)
    grad_second = from_relative(back_rel(up_low, w_up), order_tokens)
    grad_middle, grad_second_gain = second_back(grad_second)
    grad_middle = grad_middle + upstream
    grad_middle, up_wait = tie(grad_middle, up_wait)
    up_wait = sum_up.send(up_wait)
    branch_low = grad_middle.astype(jnp.bfloat16)
    sum_branch = owed(branch_rel, branch_low, lines, False)
    branch_wait = next(sum_branch)
    grad_branch = from_relative(back_rel(branch_low, w_branch), order_branch)
    grad_gated = grad_branch[:, :inner]
    grad_attn = grad_branch[:, inner:]
    grad_ssm, grad_zgate, grad_mixer_gain = gated_back(grad_gated)
    zgate_low = grad_zgate.astype(jnp.bfloat16)
    grad_ssm, down_wait = tie(grad_ssm, down_wait)
    grad_down = sum_down.send(down_wait)
    value_grad, grad_incoming, row_sum, col_sum, write_grad, read_grad = ssd_back(
        grad_ssm, filtered_low, running, run_rows, stride_rows, entering, skip_gain, start_rows,
        seg_col, seg_row,
    )
    packed_grad = packed_message(grad_incoming, carry_decay)
    later_grads = [from_earlier(packed_grad, -d) for d in range(1, pieces)]
    grad_attn, branch_wait, value_grad = tie(grad_attn, branch_wait, value_grad)
    branch_wait = sum_branch.send(branch_wait)
    query_low, key_part, value_part = attention_back(queries, grad_attn, lse, all_keys, places)
    keys_part = jnp.concatenate([key_part, value_part], axis=1)
    keys_total = keys_part[:local_len]
    for d in range(1, pieces):
        sent = keys_part[d * local_len : (d + 1) * local_len].astype(jnp.bfloat16)
        keys_total = keys_total + from_earlier(sent, -d).astype(jnp.float32)
    key_total = keys_total[:, :key_width]
    value_total = keys_total[:, key_width:]
    key_low = turn_pair(key_total, cosine, -sine).astype(jnp.bfloat16)
    value_low = value_total.astype(jnp.bfloat16)
    mix_low = jnp.concatenate([zgate_low, query_low, key_low, value_low], axis=1)
    sum_mix = owed(normed_rel, mix_low, lines, False)
    mix_wait = next(sum_mix)
    grad_skip = jnp.sum(
        jnp.sum(grad_ssm * filtered_low[:, :inner].astype(jnp.float32), axis=0).reshape(
            SSM_HEADS, SSM_HEAD
        ),
        axis=1,
    )
    value_grad, end_grad, write_grad, decay_grad = ssd_state_back(
        filtered_low, end_weights, value_grad, write_grad, start_rows, later_grads
    )
    grad_decay_total = decay_grad[0]
    col_part = col_sum.T
    ended = end_grad * end_weights
    grad_running = row_sum - stride * col_part - ended
    grad_final = jnp.sum(ended, axis=0) + grad_decay_total * carry_decay
    last_row = (jnp.arange(local_len) == local_len - 1).astype(jnp.float32)[:, None]
    grad_logs = later_sum(grad_running + last_row * grad_final[None, :])
    grad_stride = col_part + end_grad * end_decay + grad_logs * rate
    grad_step = grad_stride * jax.nn.sigmoid(stride_in)
    grad_decay_log = rate * jnp.sum(grad_logs * stride, axis=0)
    grad_step_bias = jnp.sum(grad_step, axis=0)
    xc_grad = jnp.concatenate([value_grad, write_grad, read_grad], axis=1)
    xc_grad, up_wait, mix_wait = tie(xc_grad, up_wait, mix_wait)
    grad_ups = sum_up.send(up_wait)
    mix_wait = sum_mix.send(mix_wait)
    grad_ext, grad_taps, grad_fbias = filter_back(xc_grad)
    returned = passed_along(grad_ext[: CONV - 1], "seq", -1)
    grad_mixed = grad_ext[CONV - 1 :] + jnp.pad(returned, ((local_len - CONV + 1, 0), (0, 0)))
    step_pad_low = jnp.pad(grad_step.astype(jnp.bfloat16), ((0, 0), (0, 128 - SSM_HEADS)))
    input_low = jnp.concatenate([grad_mixed.astype(jnp.bfloat16), step_pad_low], axis=1)
    input_low, branch_wait = tie(input_low, branch_wait)
    grad_branch_rows = sum_branch.send(branch_wait)
    sum_input = owed(normed_rel, input_low, lines, True)
    input_wait = next(sum_input)
    input_wait = sum_input.send(input_wait)
    mix_wait, input_wait = tie(mix_wait, input_wait)
    grad_mix = sum_mix.send(mix_wait)
    grad_normed = from_relative(
        back_rel(input_low, w_input) + back_rel(mix_low, w_mix), order_tokens
    )
    input_wait = sum_input.send(input_wait)
    grad_inputs = sum_input.send(input_wait)
    mixer_rows = mixer_output.shape[0]
    mixer_grads = (
        grad_mix[:, :inner],
        grad_inputs[:, :conv_width],
        grad_inputs[:, conv_width : conv_width + SSM_HEADS],
        grad_branch_rows[:mixer_rows],
        grad_mix[:, inner : inner + query_width],
        grad_mix[:, inner + query_width : inner + query_width + key_width],
        grad_mix[:, inner + query_width + key_width :],
        grad_branch_rows[mixer_rows:],
    )
    ffn_grads = (grad_ups[:, : gate_weight.shape[1]], grad_ups[:, gate_weight.shape[1] :], grad_down)
    grad_tokens, grad_input_gain = norm_back(grad_normed)
    grad_tokens = grad_tokens + grad_middle
    small = (
        grad_input_gain,
        grad_second_gain,
        grad_mixer_gain,
        grad_taps,
        grad_fbias,
        grad_decay_log,
        grad_step_bias,
        grad_skip,
    )
    sizes = [part.size for part in small]
    length = sum(sizes)
    flat = jnp.pad(
        jnp.concatenate([part.reshape(-1) for part in small]), (0, -length % 1024)
    ).reshape(-1, 128)
    flat = sum_everywhere(flat).reshape(-1)
    small_sums = []
    start = 0
    for part in small:
        small_sums.append(flat[start : start + part.size].reshape(part.shape))
        start += part.size
    return (
        result[None],
        grad_tokens[None],
        mixer_grads[0],
        mixer_grads[1],
        mixer_grads[2],
        mixer_grads[3],
        mixer_grads[4],
        mixer_grads[5],
        mixer_grads[6],
        mixer_grads[7],
        ffn_grads[0],
        ffn_grads[1],
        ffn_grads[2],
        small_sums[0],
        small_sums[1],
        small_sums[2],
        small_sums[3],
        small_sums[4],
        small_sums[5],
        small_sums[6],
        small_sums[7],
    )


def solution(mesh):
    placed = (
        P("dp", "seq", None),
        P("dp", None),
        P("dp", "seq", None),
        P(("dp", "seq"), None),
        P(("dp", "seq"), None),
        P(("dp", "seq"), None),
        P(("dp", "seq"), None),
        P(("dp", "seq"), None),
        P(("dp", "seq"), None),
        P(("dp", "seq"), None),
        P(("dp", "seq"), None),
        P(("dp", "seq"), None),
        P(("dp", "seq"), None),
        P(("dp", "seq"), None),
        P(),
        P(),
        P(),
        P(),
        P(),
        P(),
        P(),
        P(),
    )
    return jax.shard_map(
        body,
        mesh=mesh,
        in_specs=placed,
        out_specs=(
            P("dp", "seq", None),
            P("dp", "seq", None),
            P(("dp", "seq"), None),
            P(("dp", "seq"), None),
            P(("dp", "seq"), None),
            P(("dp", "seq"), None),
            P(("dp", "seq"), None),
            P(("dp", "seq"), None),
            P(("dp", "seq"), None),
            P(("dp", "seq"), None),
            P(("dp", "seq"), None),
            P(("dp", "seq"), None),
            P(("dp", "seq"), None),
            P(),
            P(),
            P(),
            P(),
            P(),
            P(),
            P(),
            P(),
        ),
        check_vma=False,
    )
```
